32 devices in a mesh: groups: 2 (over x), gx: 8 (over z, y), gy: 2 (over core).
Axes of the slice: x: 2, y: 2, z: 4, core: 2. Of those that a mesh axis runs over, the one named last changes fastest.
Arguments:
- fixed: bfloat16 [1024, 256, 128], P(('groups', 'gx'), 'gy'), parts along dimension 0, may hold values from -6 to 6
- moving: bfloat16 [1024, 256, 128], P(('groups', 'gx'), 'gy'), parts along dimension 0, may hold values from -6 to 6
- source_x: int32 [4, 8, 4, 2], P('groups'), parts along dimension 0, may hold values from 0 to 7, as said below
- source_z: int32 [4, 8, 4, 2], P('groups'), parts along dimension 0, may hold values from 0 to 1
Outputs:
- field: float32 [3, 1024, 256, 128], P(None, ('groups', 'gx'), 'gy'), parts along dimension 1
- mismatch: float32 [1024, 256, 128], P(('groups', 'gx'), 'gy'), parts along dimension 0
The draws below stay inside these ranges and needn't reach their ends.
There are 2 independent parts, one for each index of `groups`. The reference program is written for one: setup_inputs(seed, part) draws one part's arguments, and reference() takes and returns one part's arrays. A program takes and returns all parts, laid end to end along the dimension named above; each array names one. Nothing has to cross between parts.
Inputs may be any that keep to these rules, and one draw needn't show every extreme that they name: `source_x`: in every iteration, the 4 target blocks that share one x index and one aligned group of 2 y indices (b from 2 * g to 2 * g + 1) name different source x indices.
All inputs are finite; a program needn't handle non-finite values.
Results may differ from the reference program's by a relative error of at most 0.0003.
Values may be sent and summed in bfloat16 or wider, within the bound.
No kernel may reach another device: no remote copies, remote signals or barrier semaphores. Data moves between devices by JAX's collectives and lax.ppermute only.
A program may use at most 256 MiB of HBM per device.

```python
import jax
import jax.numpy as jnp
from jax import lax

BLK = 64
YB = 2
ZB = 2
ITERS = 2
RADIUS = 4
NX = 512
NY = 256
NZ = 128
N_GX = 8
N_GY = 2


def draw_source_x(key, part):
    key = jax.random.fold_in(key, 11)
    hot_key, noise_key, order_key = jax.random.split(key, 3)
    per_group = YB * ZB
    hot_flag = jax.random.randint(hot_key, (ITERS, 1, 1, N_GX), 0, 4)
    popular = jnp.where(hot_flag == 0, 3000, 0)
    noise = jax.random.randint(noise_key, (ITERS, N_GX, N_GY, N_GX), 0, 4096)
    target = jnp.arange(N_GX, dtype=jnp.int32)[None, :, None, None]
    source = jnp.arange(N_GX, dtype=jnp.int32)[None, None, None, :]
    scores = (noise + popular - 400 * jnp.abs(source - target)) * N_GX + source
    picks = lax.top_k(scores, per_group)[1]
    shuffle = jax.random.randint(order_key, (ITERS, N_GX, N_GY, per_group), 0, 4096) * per_group + jnp.arange(per_group, dtype=jnp.int32)
    order = lax.top_k(shuffle, per_group)[1]
    picks = jnp.take_along_axis(picks, order, axis=3)
    return picks.reshape(ITERS, N_GX, N_GY * YB, ZB).astype(jnp.int32)


def touch_ends(entries, own_key, least, high):
    shape = entries.shape
    index_at = [jax.random.randint(jax.random.fold_in(own_key, axis), (), 0, shape[axis]) for axis in range(len(shape))]
    entries = entries.at[tuple(index_at)].set(least)
    longest = shape.index(max(shape))
    index_at[longest] = (index_at[longest] + 1) % shape[longest]
    return entries.at[tuple(index_at)].set(high)


def levels(key, dims, cuts, low, high):
    factor_of = 1.0
    for position, parts in cuts:
        draws = jax.random.uniform(jax.random.fold_in(jax.random.fold_in(key, 6), position), (parts,), jnp.float32, low / len(cuts), high / len(cuts))
        factor_of = factor_of * jnp.repeat(jnp.exp(draws), dims[position] // parts).reshape((-1,) + (1,) * (len(dims) - 1 - position))
    return factor_of


def scatter_about(stream_key, dims, deviation, most, cuts=(), kind=jnp.bfloat16):
    entries = deviation * jax.random.normal(stream_key, dims, jnp.float32)
    if cuts:
        entries = entries * levels(stream_key, dims, cuts, -0.22, 0.18)
    return jnp.clip(entries, -most, most).astype(kind)


def setup_inputs(seed: int = 0, part: int = 0) -> dict:
    key_of = jax.random.split(jax.random.key(seed), 5)
    part_splits = jax.random.split(jax.random.fold_in(key_of[4], part), 5)
    return {
        "fixed": scatter_about(part_splits[0], (NX, NY, NZ), 1.0, 6.0, ((0, 8), (1, 2))),
        "moving": scatter_about(part_splits[1], (NX, NY, NZ), 1.0, 6.0, ((0, 8), (1, 2))),
        "source_x": draw_source_x(jax.random.fold_in(jax.random.fold_in(key_of[4], part), 71), part),
        "source_z": touch_ends(jax.random.randint(part_splits[3], (ITERS, N_GX, YB * N_GY, ZB), 0, ZB), jax.random.fold_in(part_splits[3], 1), 0, ZB - 1).astype(jnp.int32),
    }


STIFF = 0.05


def gauss_taps():
    offsets = jnp.arange(-RADIUS, RADIUS + 1).astype(jnp.float32)
    weights = jnp.exp(-offsets * offsets / 4.5)
    return weights / jnp.sum(weights)


def tent_weight(offset):
    return jnp.maximum(0.0, 1.0 - jnp.abs(offset))


def warp_block(source, displace):
    source = source.astype(jnp.float32)
    extent = displace.shape[1]
    result = jnp.zeros(displace.shape[1:], jnp.float32)
    for shift_x in (-1, 0, 1):
        weight_x = tent_weight(displace[0] - shift_x)
        for shift_y in (-1, 0, 1):
            weight_xy = weight_x * tent_weight(displace[1] - shift_y)
            for shift_z in (-1, 0, 1):
                weight = weight_xy * tent_weight(displace[2] - shift_z)
                starts = (2 + shift_x, 2 + shift_y, 2 + shift_z)
                section = lax.slice(source, starts, (starts[0] + extent, starts[1] + extent, starts[2] + extent))
                result = result + weight * section
    return result


def central(padded):
    along_x = (padded[2:, 1:-1, 1:-1] - padded[:-2, 1:-1, 1:-1]) * 0.5
    along_y = (padded[1:-1, 2:, 1:-1] - padded[1:-1, :-2, 1:-1]) * 0.5
    along_z = (padded[1:-1, 1:-1, 2:] - padded[1:-1, 1:-1, :-2]) * 0.5
    return jnp.stack([along_x, along_y, along_z])


def filter_padded(padded, axis_pos, length, kernel_taps):
    result = kernel_taps[0] * lax.slice_in_dim(padded, 0, length, axis=axis_pos)
    for offset in range(1, 2 * RADIUS + 1):
        result = result + kernel_taps[offset] * lax.slice_in_dim(padded, offset, offset + length, axis=axis_pos)
    return result


def smooth_along(values, axis_pos, kernel_taps):
    widths = [(0, 0)] * values.ndim
    widths[axis_pos] = (RADIUS, RADIUS)
    return filter_padded(jnp.pad(values, widths), axis_pos, values.shape[axis_pos], kernel_taps)


def reference(fixed, moving, source_x, source_z):
    blocks_x = NX // BLK
    blocks_y = NY // BLK
    block_count = blocks_x * blocks_y * ZB
    extent = BLK + 4
    kernel_taps = gauss_taps()
    fixed_float = fixed.astype(jnp.float32)
    grad_fixed = central(jnp.pad(fixed_float, 1))
    moving_pad = jnp.pad(moving, 2)
    field = jnp.zeros((3, NX, NY, NZ), jnp.float32)
    mismatch = jnp.zeros((NX, NY, NZ), jnp.float32)
    for segment in range(ITERS):
        def one_block(block_id, segment=segment, field=field):
            block_x = block_id // (blocks_y * ZB)
            block_y = (block_id // ZB) % blocks_y
            block_z = block_id % ZB
            src_col = source_x[segment, block_x, block_y, block_z]
            src_depth = source_z[segment, block_x, block_y, block_z]
            starts = [(src_col * BLK).astype(jnp.int32), (block_y * BLK).astype(jnp.int32), (src_depth * BLK).astype(jnp.int32)]
            source = lax.dynamic_slice(moving_pad, starts, (extent, extent, extent))
            corner = [jnp.int32(0), (block_x * BLK).astype(jnp.int32), (block_y * BLK).astype(jnp.int32), (block_z * BLK).astype(jnp.int32)]
            displace = lax.dynamic_slice(field, corner, (3, BLK, BLK, BLK))
            return warp_block(source, displace)
        blocks = lax.map(one_block, jnp.arange(block_count).astype(jnp.int32))
        warped = blocks.reshape(blocks_x, blocks_y, ZB, BLK, BLK, BLK).transpose(0, 3, 1, 4, 2, 5).reshape(NX, NY, NZ)
        mismatch = fixed_float - warped
        mean_grad = 0.5 * (grad_fixed + central(jnp.pad(warped, 1)))
        denominator = jnp.sum(mean_grad * mean_grad, axis=0) + mismatch * mismatch + STIFF
        summed = field + mismatch * mean_grad / denominator
        for axis_pos in (1, 2, 3):
            summed = smooth_along(summed, axis_pos, kernel_taps)
        field = summed
    return field, mismatch
```

```python
import functools

import jax
import jax.numpy as jnp
import numpy as np
from jax import lax
from jax.experimental import pallas as pl
from jax.experimental.pallas import tpu as pltpu
from jax.sharding import PartitionSpec as P

BLK = 64
RADIUS = 4
STIFF = 0.05
LANES = 128
CH = 8
LIMIT = 56 * 1024 * 1024
F32 = jnp.float32
BF16 = jnp.bfloat16


def taps():
    k = np.arange(-RADIUS, RADIUS + 1).astype(np.float32)
    w = np.exp(-k * k / np.float32(4.5)).astype(np.float32)
    return (w / np.sum(w)).astype(np.float32)


def band():
    w = taps()
    full = np.zeros((LANES, LANES), np.float32)
    for i in range(LANES):
        for k in range(-RADIUS, RADIUS + 1):
            if 0 <= i + k < LANES:
                full[i + k, i] = w[k + RADIUS]
    high = jnp.asarray(full).astype(BF16)
    low = (jnp.asarray(full) - high.astype(F32)).astype(BF16)
    row = jnp.concatenate([high, low], 1)
    return jnp.concatenate([row, row], 0)


def swap_halves(x):
    return pltpu.roll(x.astype(F32), 64, x.ndim - 1).astype(x.dtype)


def lane_of(shape):
    return lax.broadcasted_iota(jnp.int32, shape, len(shape) - 1)


class Table:
    def __init__(self, shape):
        self.shape = shape
        self.size = int(np.prod(shape))

    def at(self, t, d, b, c):
        _, n, yb, zb = self.shape
        return ((t * n + d) * yb + b) * zb + c

    def x(self, ref, t, d, b, c):
        return ref[self.at(t, d, b, c)]

    def z(self, ref, t, d, b, c):
        return ref[self.size + self.at(t, d, b, c)]

    def column(self, ref):
        return ref[2 * self.size]

    def row(self, ref):
        return ref[2 * self.size + 1]


def wanted_block(table, ref, t, d):
    a, g = table.column(ref), table.row(ref)
    blk_y, blk_z = jnp.int32(0), jnp.int32(0)
    for b in range(2):
        for c in range(2):
            hit = table.x(ref, t, d, g * 2 + b, c) == a
            blk_y = jnp.where(hit, b, blk_y)
            blk_z = jnp.where(hit, table.z(ref, t, d, g * 2 + b, c), blk_z)
    return blk_y, blk_z


def pack_body(table, t, shell, ref, mov, *refs):
    d = pl.program_id(0)
    blk_y, blk_z = wanted_block(table, ref, t, d)
    if shell:
        shells, out = refs
    else:
        (out,) = refs
    y0 = pl.multiple_of(blk_y * BLK, BLK)
    keep = (lane_of((BLK, LANES)) < 64) == (blk_z == 0)

    def step(x, carry):
        same = mov[x + 32 * blk_z, pl.ds(y0, BLK), :].astype(F32)
        other = mov[x + 32 * (1 - blk_z), pl.ds(y0, BLK), :].astype(F32)
        got = jnp.where(keep, same, pltpu.roll(other, 64, 1)).astype(BF16)
        out[0, pl.ds(pl.multiple_of(x * BLK, BLK), BLK), :] = got
        return carry

    lax.fori_loop(0, 32, step, 0, unroll=4)
    if shell:
        out[0, 2048:, :] = shells[blk_y * 2 + blk_z]


def pack(table, tab, t, moving, shells=None):
    n = table.shape[1]
    rows = 2048 if shells is None else 2048 + shells.shape[1]
    whole = lambda nd: (lambda d, r: (0,) * nd)
    specs = [pl.BlockSpec(moving.shape, whole(3))]
    args = [moving]
    if shells is not None:
        specs.append(pl.BlockSpec(shells.shape, whole(3)))
        args.append(shells)
    return pl.pallas_call(
        functools.partial(pack_body, table, t, shells is not None),
        out_shape=jax.ShapeDtypeStruct((n, rows, LANES), BF16),
        grid_spec=pltpu.PrefetchScalarGridSpec(
            num_scalar_prefetch=1,
            grid=(n,),
            in_specs=specs,
            out_specs=pl.BlockSpec((1, rows, LANES), lambda d, r: (d, 0, 0)),
        ),
        compiler_params=pltpu.CompilerParams(vmem_limit_bytes=LIMIT),
        cost_estimate=pl.CostEstimate(flops=n * rows * 512, bytes_accessed=n * rows * 256 + 2 * moving.size, transcendentals=0),
        name="pack%d" % t,
    )(tab, *args)


def pick_body(ref, p, q, out):
    low = lane_of((BLK, LANES)) < 64

    def step(x, carry):
        a = p[0, pl.ds(pl.multiple_of(x * BLK, BLK), BLK), :].astype(F32)
        b = q[0, pl.ds(pl.multiple_of(x * BLK, BLK), BLK), :].astype(F32)
        out[x] = jnp.where(low, a, pltpu.roll(b, 64, 1)).astype(BF16)
        out[x + 32] = jnp.where(low, pltpu.roll(a, 64, 1), b).astype(BF16)
        return carry

    lax.fori_loop(0, 32, step, 0, unroll=4)


def slot_spec(table, t, c, rows):
    def where(b, *rest):
        ref = rest[-1]
        return (table.x(ref, t, table.column(ref), table.row(ref) * 2 + b, c), 0, 0)

    return pl.BlockSpec((1, rows, LANES), where)


def pick(table, tab, t, slots, shape):
    rows = slots.shape[1]
    return pl.pallas_call(
        pick_body,
        out_shape=jax.ShapeDtypeStruct(shape, BF16),
        grid_spec=pltpu.PrefetchScalarGridSpec(
            num_scalar_prefetch=1,
            grid=(2,),
            in_specs=[slot_spec(table, t, 0, rows), slot_spec(table, t, 1, rows)],
            out_specs=pl.BlockSpec((64, BLK, LANES), lambda b, r: (0, b, 0)),
        ),
        compiler_params=pltpu.CompilerParams(vmem_limit_bytes=LIMIT),
        cost_estimate=pl.CostEstimate(flops=2 * 64 * 128 * 128, bytes_accessed=8 << 20, transcendentals=0),
        name="pick",
    )(tab, slots, slots)


XC = 16


def warp_body(table, t, ref, p, q, fixed, field, out, near, up, down, edge):
    b, chunk = pl.program_id(0), pl.program_id(1)

    @pl.when(chunk == 0)
    def _():
        low = lane_of((BLK, LANES)) < 64

        def both(rows, size):
            a = p[0, pl.ds(rows, size), :].astype(F32)
            c = q[0, pl.ds(rows, size), :].astype(F32)
            mask = low if size == BLK else lane_of((size, LANES)) < 64
            return (
                jnp.where(mask, a, pltpu.roll(c, 64, 1)),
                jnp.where(mask, pltpu.roll(a, 64, 1), c),
            )

        def step(x, carry):
            first, second = both(pl.multiple_of(x * BLK, BLK), BLK)
            near[x + 1, 8:72, :] = first
            near[x + 33, 8:72, :] = second
            return carry

        lax.fori_loop(0, 32, step, 0, unroll=2)
        first, second = both(2048, BLK)
        near[0, 8:72, :] = first
        near[65, 8:72, :] = second
        first, second = both(2112, 80)
        edge[0] = first
        edge[1] = second

        a, g = table.column(ref), table.row(ref)
        spot_p = jnp.where(table.z(ref, t, a, g * 2 + b, 0) == 0, 63, 0)
        spot_q = jnp.where(table.z(ref, t, a, g * 2 + b, 1) == 0, 127, 64)
        face_p = p[0, 2192:2272, :].astype(F32)
        face_q = q[0, 2192:2272, :].astype(F32)
        lane = lane_of((80, LANES))

        def widen(i, carry):
            near[i, 7:8, :] = edge[0, pl.ds(i, 1), :]
            near[i, 72:73, :] = edge[1, pl.ds(i, 1), :]
            value = near[i]
            at_p = pltpu.roll(face_p, lax.rem(spot_p - i + 256, 128), 1)
            at_q = pltpu.roll(face_q, lax.rem(spot_q - i + 256, 128), 1)
            fill = jnp.where(lane == spot_p, at_p, jnp.where(lane == spot_q, at_q, 0.0))
            up[i] = jnp.where((lane == 63) | (lane == 127), fill, pltpu.roll(value, 127, 1))
            down[i] = jnp.where((lane == 0) | (lane == 64), fill, pltpu.roll(value, 1, 1))
            return carry

        lax.fori_loop(0, 66, widen, 0)

    def plane(x, carry):
        xi = chunk * XC + x
        for tile in range(8):
            r = 8 * tile
            fx, fy, fz = field[0, x, r : r + 8, :], field[1, x, r : r + 8, :], field[2, x, r : r + 8, :]
            px, py, pz = fx > 0, fy > 0, fz > 0
            wx, wy, wz = jnp.abs(fx), jnp.abs(fy), jnp.abs(fz)
            per_x = []
            for kx in range(3):
                per_y = []
                for ky in range(3):
                    y0 = 7 + r + ky
                    here = near[xi + kx, y0 : y0 + 8, :]
                    beside = jnp.where(pz, up[xi + kx, y0 : y0 + 8, :], down[xi + kx, y0 : y0 + 8, :])
                    per_y.append((here, beside))
                far = [jnp.where(py, per_y[2][i], per_y[0][i]) for i in range(2)]
                per_x.append((per_y[1], far))
            corner = [
                [
                    per_x[1][j][i] if s == 0 else jnp.where(px, per_x[2][j][i], per_x[0][j][i])
                    for j in range(2)
                    for i in range(2)
                ]
                for s in range(2)
            ]
            lines = []
            for s in range(2):
                c00, c01, c10, c11 = corner[s]
                l0 = c00 + wz * (c01 - c00)
                l1 = c10 + wz * (c11 - c10)
                lines.append(l0 + wy * (l1 - l0))
            warped = lines[0] + wx * (lines[1] - lines[0])
            out[x, r : r + 8, :] = fixed[x, r : r + 8, :].astype(F32) - warped
        return carry

    lax.fori_loop(0, XC, plane, 0)


def warp(table, tab, t, slots, fixed, field):
    rows = slots.shape[1]
    tile_x, tile_y, tile_z = fixed.shape

    block = pl.BlockSpec((XC, BLK, LANES), lambda b, c, r: (c, b, 0))
    return pl.pallas_call(
        functools.partial(warp_body, table, t),
        out_shape=jax.ShapeDtypeStruct(fixed.shape, F32),
        grid_spec=pltpu.PrefetchScalarGridSpec(
            num_scalar_prefetch=1,
            grid=(2, tile_x // XC),
            in_specs=[
                slot_spec(table, t, 0, rows),
                slot_spec(table, t, 1, rows),
                block,
                pl.BlockSpec((3, XC, BLK, LANES), lambda b, c, r: (0, c, b, 0)),
            ],
            out_specs=block,
            scratch_shapes=[pltpu.VMEM((66, 80, LANES), F32)] * 3 + [pltpu.VMEM((2, 80, LANES), F32)],
        ),
        compiler_params=pltpu.CompilerParams(vmem_limit_bytes=LIMIT),
        cost_estimate=pl.CostEstimate(flops=60 << 20, bytes_accessed=22 << 20, transcendentals=0),
        name="warp",
    )(tab, slots, slots, fixed, field)


def put_planes(is_warped, g, count, start, total, diff, value, value_y, fixed, fixed_y):
    def step(i, carry):
        f, v = fixed[i].astype(F32), value[i].astype(F32)
        fy, vy = fixed_y[i].astype(F32), value_y[i].astype(F32)
        fy = jnp.where(g == 1, fy[8:16], fy[0:8])
        if vy.shape[0] == 16:
            vy = jnp.where(g == 1, vy[8:16], vy[0:8])
        if is_warped:
            s, m, sy, my = f + v, f - v, fy + vy, fy - vy
        else:
            s, m, sy, my = 2.0 * f - v, v, 2.0 * fy - vy, vy
        zero = jnp.zeros_like(sy)
        j = start + i
        total[j, 16:144, :] = s
        diff[j, 16:144, :] = m
        total[j, 8:16, :] = jnp.where(g == 1, sy, zero)
        total[j, 144:152, :] = jnp.where(g == 0, sy, zero)
        diff[j, 8:16, :] = jnp.where(g == 1, my, zero)
        diff[j, 144:152, :] = jnp.where(g == 0, my, zero)
        return carry

    lax.fori_loop(0, count, step, 0)


def update_planes(g, count, base, start, total, diff, summed, prior, prior_y, source):
    lane = lane_of((8, LANES))

    def step(i, carry):
        j = start + i
        for t in range(18):
            r = 8 + 8 * t
            here = total[j, r : r + 8, :]
            gx = total[j + 1, r : r + 8, :] - total[j - 1, r : r + 8, :]
            gy = total[j, r + 1 : r + 9, :] - total[j, r - 1 : r + 7, :]
            gz = jnp.where(lane < LANES - 1, pltpu.roll(here, LANES - 1, 1), 0.0) - jnp.where(
                lane > 0, pltpu.roll(here, 1, 1), 0.0
            )
            m = diff[j, r : r + 8, :]
            size = (gx * gx + gy * gy) + (gz * gz + (16.0 * m * m + 16.0 * STIFF))
            inv = pl.reciprocal(size, approx=True)
            inv = inv * (2.0 - size * inv)
            scale = (4.0 * m) * inv
            for c, grad in enumerate((gx, gy, gz)):
                value = scale * grad
                if prior is not None:
                    if 1 <= t <= 16:
                        value = value + prior[c, source + i, 8 * t - 8 : 8 * t, :]
                    else:
                        own = (g == 1) if t == 0 else (g == 0)
                        value = value + jnp.where(own, prior_y[c, source + i, 0:8, :], 0.0)
                summed[c, base + i, r - 8 : r, :] = value
        return carry

    lax.fori_loop(0, count, step, 0)


def smooth_planes(before, after, summed, along, wide, weights, out):
    w = [float(v) for v in taps()]

    def tap_sum(values):
        acc = w[RADIUS] * values[RADIUS]
        for k in range(RADIUS):
            acc = acc + w[k] * (values[k] + values[2 * RADIUS - k])
        return acc

    def rows(t, carry):
        r = pl.ds(pl.multiple_of(8 * t, 8), 8)
        for c in range(3):
            planes = [summed[c, before + j, r, :] for j in range(CH)]
            planes += [summed[c, after + j, r, :] for j in range(CH)]
            for o in range(CH):
                along[c, o, r, :] = tap_sum(planes[o : o + 2 * RADIUS + 1])
        return carry

    lax.fori_loop(0, 18, rows, 0)

    def plane(o, carry):
        for c in range(3):
            for t in range(8):
                r = 16 * t + 4
                acc = tap_sum([along[c, o, r + k : r + k + 16, :] for k in range(2 * RADIUS + 1)])
                high = acc.astype(BF16)
                wide[c * 128 + 16 * t : c * 128 + 16 * t + 16, 0:LANES] = high
                wide[c * 128 + 16 * t : c * 128 + 16 * t + 16, LANES:] = (acc - high.astype(F32)).astype(BF16)
        got = jnp.dot(wide[...], weights[...], preferred_element_type=F32)
        for c in range(3):
            part = got[c * 128 : c * 128 + 128]
            out[c, o] = part[:, :LANES] + part[:, LANES:]
        return carry

    lax.fori_loop(0, CH, plane, 0)


def scratch(planes):
    return [
        pltpu.VMEM((planes, 160, LANES), F32),
        pltpu.VMEM((planes, 160, LANES), F32),
        pltpu.VMEM((3, 16, 144, LANES), F32),
        pltpu.VMEM((3, CH, 144, LANES), F32),
        pltpu.VMEM((384, 256), BF16),
    ]


def inner_body(table, is_warped, ref, weights, value, value_y, fixed, fixed_y, *refs):
    prior, prior_y = (None, None) if is_warped else refs[:2]
    out, total, diff, summed, along, wide = refs[0 if is_warped else 2 :]
    k = pl.program_id(0)
    g = table.row(ref)
    cur = lax.rem(k, 2) * CH
    put_planes(is_warped, g, CH + 2, 0, total, diff, value, value_y, fixed, fixed_y)
    update_planes(g, CH, cur, 1, total, diff, summed, prior, prior_y, 0)

    @pl.when(k > 0)
    def _():
        smooth_planes(CH - cur, cur, summed, along, wide, weights, out)


def inner(table, tab, weights, value, value_y, fixed, fixed_y, prior=None, prior_y=None):
    tile_x = fixed.shape[0]
    is_warped = prior is None

    def window(array, planes, first):
        dims = array.shape
        if len(dims) == 3:
            return pl.BlockSpec(
                (pl.Element(planes), pl.Element(dims[1]), pl.Element(dims[2])), lambda k, r: (k * CH + first, 0, 0)
            )
        return pl.BlockSpec(
            (pl.Element(dims[0]), pl.Element(planes), pl.Element(dims[2]), pl.Element(dims[3])),
            lambda k, r: (0, k * CH + first, 0, 0),
        )

    specs = [pl.BlockSpec(weights.shape, lambda k, r: (0, 0))]
    args = [weights]
    for array in (value, value_y, fixed, fixed_y):
        specs.append(window(array, CH + 2, 3))
        args.append(array)
    if not is_warped:
        for array in (prior, prior_y):
            specs.append(window(array, CH, 4))
            args.append(array)
    return pl.pallas_call(
        functools.partial(inner_body, table, is_warped),
        out_shape=jax.ShapeDtypeStruct((3,) + fixed.shape, F32),
        grid_spec=pltpu.PrefetchScalarGridSpec(
            num_scalar_prefetch=1,
            grid=(tile_x // CH - 1,),
            in_specs=specs,
            out_specs=pl.BlockSpec((3, CH) + fixed.shape[1:], lambda k, r: (0, jnp.maximum(k, 1), 0, 0)),
            scratch_shapes=scratch(CH + 2),
        ),
        compiler_params=pltpu.CompilerParams(vmem_limit_bytes=LIMIT),
        cost_estimate=pl.CostEstimate(flops=200 << 20, bytes_accessed=30 << 20, transcendentals=0),
        name="inner%d" % (not is_warped),
    )(tab, *args)


def rim_body(table, is_warped, ref, weights, value, value_y, fixed, fixed_y, *refs):
    halo = refs[:4]
    refs = refs[4:]
    if is_warped:
        prior = prior_y = None
    else:
        prior, prior_y, prior_low, prior_high = refs[:4]
        refs = refs[4:]
    _, out, total, diff, summed, along, wide = refs
    k = pl.program_id(0)
    g = table.row(ref)
    put_planes(is_warped, g, 13, 5 * (1 - k), total, diff, value, value_y, fixed, fixed_y)

    def side(at, value_x, fixed_x):
        v_main, v_y = value_x.at[:, :128, :], value_x.at[:, 128:, :]
        f_main, f_y = fixed_x.at[:, :128, :], fixed_x.at[:, 128:, :]
        put_planes(is_warped, g, 5, at, total, diff, v_main, v_y, f_main, f_y)

    @pl.when(k == 0)
    def _():
        side(0, halo[0], halo[2])

    @pl.when(k == 1)
    def _():
        side(13, halo[1], halo[3])

    if is_warped:
        update_planes(g, 16, 0, 1, total, diff, summed, None, None, 0)
    else:
        update_planes(g, 12, 4 * (1 - k), 1 + 4 * (1 - k), total, diff, summed, prior, prior_y, 0)

        def outside(at, prior_x):
            update_planes(
                g, 4, at, 1 + at, total, diff, summed, prior_x.at[:, :, :128, :], prior_x.at[:, :, 128:, :], 0
            )

        @pl.when(k == 0)
        def _():
            outside(0, prior_low)

        @pl.when(k == 1)
        def _():
            outside(12, prior_high)

    smooth_planes(0, CH, summed, along, wide, weights, out)


def rim(table, tab, weights, field, value, value_y, fixed, fixed_y, halo, prior=None, prior_y=None, prior_x=()):
    tile_x = fixed.shape[0]
    is_warped = prior is None

    def window(array, planes):
        dims = array.shape
        if len(dims) == 3:
            return pl.BlockSpec(
                (pl.Element(planes), pl.Element(dims[1]), pl.Element(dims[2])),
                lambda k, r: (k * (tile_x - planes), 0, 0),
            )
        return pl.BlockSpec(
            (pl.Element(dims[0]), pl.Element(planes), pl.Element(dims[2]), pl.Element(dims[3])),
            lambda k, r: (0, k * (tile_x - planes), 0, 0),
        )

    def whole(array):
        return pl.BlockSpec(array.shape, lambda k, r: (0,) * array.ndim)

    specs, args = [whole(weights)], [weights]
    for array in (value, value_y, fixed, fixed_y):
        specs.append(window(array, 13))
        args.append(array)
    for array in halo:
        specs.append(whole(array))
        args.append(array)
    if not is_warped:
        for array in (prior, prior_y):
            specs.append(window(array, 12))
            args.append(array)
        for array in prior_x:
            specs.append(whole(array))
            args.append(array)
    specs.append(pl.BlockSpec(memory_space=pl.ANY))
    args.append(field)
    last = tile_x // CH - 1
    return pl.pallas_call(
        functools.partial(rim_body, table, is_warped),
        out_shape=jax.ShapeDtypeStruct(field.shape, F32),
        grid_spec=pltpu.PrefetchScalarGridSpec(
            num_scalar_prefetch=1,
            grid=(2,),
            in_specs=specs,
            out_specs=pl.BlockSpec((3, CH) + fixed.shape[1:], lambda k, r: (0, k * last, 0, 0)),
            scratch_shapes=scratch(18),
        ),
        input_output_aliases={len(args): 0},
        compiler_params=pltpu.CompilerParams(vmem_limit_bytes=LIMIT),
        cost_estimate=pl.CostEstimate(flops=60 << 20, bytes_accessed=10 << 20, transcendentals=0),
        name="rim%d" % (not is_warped),
    )(tab, *args)


def swap_y(value, g, rows):
    length = value.shape[-2]
    first = lax.slice_in_dim(value, 0, rows, axis=value.ndim - 2)
    last = lax.slice_in_dim(value, length - rows, length, axis=value.ndim - 2)
    return lax.ppermute(jnp.where(g == 0, last, first), "gy", [(0, 1), (1, 0)])


def shift_x(value, value_y, width):
    size = lax.axis_size("gx")
    axis = value.ndim - 3
    length = value.shape[axis]
    up = [(i, i + 1) for i in range(size - 1)]
    down = [(j, i) for i, j in up]

    def part(start):
        return jnp.concatenate(
            [lax.slice_in_dim(v, start, start + width, axis=axis) for v in (value, value_y)], axis=value.ndim - 2
        )

    return lax.ppermute(part(length - width), "gx", up), lax.ppermute(part(0), "gx", down)


def shell_rows(moving, moving_y, low, high, g):
    last, first = moving_y.shape[1] - 1, 0

    def extend(main, rows_y):
        below = jnp.where(g == 1, rows_y[:, last : last + 1], 0)
        above = jnp.where(g == 0, rows_y[:, first : first + 1], 0)
        return jnp.concatenate([below, main, above], axis=1)

    planes = jnp.concatenate([low[:, :128], moving, high[:, :128]], axis=0)
    planes_y = jnp.concatenate([low[:, 128:], moving_y, high[:, 128:]], axis=0)
    ext = extend(planes, planes_y)
    faces = []
    for b in range(2):
        for c in range(2):
            z = slice(c * BLK, c * BLK + BLK)
            y = slice(b * BLK + 1, b * BLK + 1 + BLK)
            side_x = jnp.concatenate([ext[0, y, z], ext[65, y, z]], axis=1)
            side_y = jnp.concatenate([ext[:, b * BLK, z], ext[:, b * BLK + BLK + 1, z]], axis=1)
            side_z = ext[:, b * BLK : b * BLK + BLK + 2, BLK - c].T
            faces.append(
                jnp.concatenate(
                    [side_x, jnp.pad(side_y, ((0, 14), (0, 0))), jnp.pad(side_z, ((7, 7), (0, 62)))], axis=0
                )
            )
    return jnp.stack(faces)


def local(fixed, moving, source_x, source_z):
    g = lax.axis_index("gy")
    table = Table(source_x.shape)
    tab = jnp.concatenate(
        [
            source_x.reshape(-1),
            source_z.reshape(-1),
            jnp.stack([lax.axis_index("gx"), g]).astype(jnp.int32),
        ]
    )
    weights = band()

    def send(slots):
        return lax.all_to_all(slots, "gx", split_axis=0, concat_axis=0, tiled=True)

    slots0 = send(pack(table, tab, 0, moving))

    both = jnp.stack([fixed, moving])
    both_y = swap_y(both, g, 16)
    low, high = shift_x(both, both_y, 5)
    fixed_y = both_y[0]
    fixed_x = (low[0], high[0])
    shells = shell_rows(moving, both_y[1], low[1, 4:], high[1, :1], g)
    ready1 = pack(table, tab, 1, moving, shells)

    slots0, ready1 = lax.optimization_barrier((slots0, ready1))
    slots1 = send(ready1)

    warped = pick(table, tab, 0, slots0, fixed.shape)
    warped_y = swap_y(warped, g, 16)
    warped_x = shift_x(warped, warped_y, 5)
    field = inner(table, tab, weights, warped, warped_y, fixed, fixed_y)
    field = rim(table, tab, weights, field, warped, warped_y, fixed, fixed_y, (*warped_x, *fixed_x))
    field_y = swap_y(field, g, 8)
    field_x = shift_x(field, field_y, 4)

    mismatch = warp(table, tab, 1, slots1, fixed, field)
    mismatch_y = swap_y(mismatch, g, 8)
    mismatch_x = shift_x(mismatch, mismatch_y, 5)
    last = inner(table, tab, weights, mismatch, mismatch_y, fixed, fixed_y, field, field_y)
    last = rim(
        table, tab, weights, last, mismatch, mismatch_y, fixed, fixed_y, (*mismatch_x, *fixed_x), field, field_y, field_x
    )
    return (last, mismatch)


def solution(mesh):
    return jax.shard_map(
        local,
        mesh=mesh,
        in_specs=(
            P(("groups", "gx"), "gy", None),
            P(("groups", "gx"), "gy", None),
            P("groups", None, None, None),
            P("groups", None, None, None),
        ),
        out_specs=(P(None, ("groups", "gx"), "gy", None), P(("groups", "gx"), "gy", None)),
        check_vma=False,
    )
```

```python
import functools

import jax
import jax.numpy as jnp
import numpy as np
from jax import lax
from jax.experimental import pallas as pl
from jax.experimental.pallas import tpu as pltpu
from jax.sharding import PartitionSpec as P

BLK = 64
RADIUS = 4
STIFF = 0.05
LANES = 128
CH = 8
SMALL = pl.CostEstimate(flops=1 << 16, bytes_accessed=1 << 16, transcendentals=0)
LIMIT = 56 * 1024 * 1024
F32 = jnp.float32
BF16 = jnp.bfloat16


def taps():
    k = np.arange(-RADIUS, RADIUS + 1).astype(np.float32)
    w = np.exp(-k * k / np.float32(4.5)).astype(np.float32)
    return (w / np.sum(w)).astype(np.float32)


def band():
    w = taps()
    full = np.zeros((LANES, LANES), np.float32)
    for i in range(LANES):
        for k in range(-RADIUS, RADIUS + 1):
            if 0 <= i + k < LANES:
                full[i + k, i] = w[k + RADIUS]
    high = jnp.asarray(full).astype(BF16)
    low = (jnp.asarray(full) - high.astype(F32)).astype(BF16)
    row = jnp.concatenate([high, low], 1)
    return jnp.concatenate([row, row], 0)


def lane_of(shape):
    return lax.broadcasted_iota(jnp.int32, shape, len(shape) - 1)


class Table:
    def __init__(self, shape):
        self.shape = shape
        self.size = int(np.prod(shape))

    def at(self, t, d, b, c):
        _, n, yb, zb = self.shape
        return ((t * n + d) * yb + b) * zb + c

    def x(self, ref, t, d, b, c):
        return ref[self.at(t, d, b, c)]

    def z(self, ref, t, d, b, c):
        return ref[self.size + self.at(t, d, b, c)]

    def column(self, ref):
        return ref[2 * self.size]

    def row(self, ref):
        return ref[2 * self.size + 1]


def wanted_block(table, ref, t, d, column):
    g = table.row(ref)
    blk_y, blk_z, out_z = jnp.int32(0), jnp.int32(0), jnp.int32(0)
    for b in range(2):
        for c in range(2):
            hit = table.x(ref, t, d, g * 2 + b, c) == column
            blk_y = jnp.where(hit, b, blk_y)
            blk_z = jnp.where(hit, table.z(ref, t, d, g * 2 + b, c), blk_z)
            out_z = jnp.where(hit, c, out_z)
    return blk_y, blk_z, out_z


MAIN = 32 * BLK
GROUP = 8
PART = 32


def pack_body(table, t, far, count, shell, ref, *refs):
    n = table.shape[1]
    half = n // 2
    a = table.column(ref)
    here = (a >= half).astype(jnp.int32)
    column = a if not far else jnp.where(a >= half, a - half, a + half)
    blk_y, blk_z, out_z = wanted_block(table, ref, t, here * half + pl.program_id(0), column)
    parts, out = refs[:count], refs[-1]
    if shell:
        out = out.at[0]
    y0 = pl.multiple_of(blk_y * BLK, BLK)
    keep = (lane_of((GROUP, BLK, LANES)) < 64) == (blk_z == 0)
    turn = jnp.where(blk_z == out_z, 0, PART // 2)
    for k, mov in enumerate(parts):
        for x in range(0, PART // 2, GROUP):
            same = mov[pl.ds(x + turn, GROUP), pl.ds(y0, BLK), :]
            other = mov[pl.ds(x + PART // 2 - turn, GROUP), pl.ds(y0, BLK), :]
            other = pltpu.roll(other.reshape(GROUP * BLK, LANES), 64, 1).reshape(GROUP, BLK, LANES)
            got = jnp.where(keep, same.astype(F32), other.astype(F32)).astype(BF16)
            row = (k * PART // 2 + x) * BLK
            out[0, row : row + GROUP * BLK, :] = got.reshape(GROUP * BLK, LANES)
    if shell:
        out[0, MAIN:, :] = refs[count][blk_y * 2 + blk_z]


def pack(table, tab, t, far, parts, shells=None, into=None):
    half = table.shape[1] // 2
    args, specs = [], []
    for part in parts:
        for i in range(part.shape[0] // PART):
            args.append(part)
            specs.append(pl.BlockSpec((PART,) + part.shape[1:], lambda d, r, i=i: (i, 0, 0)))
    count = len(args)
    rows = count * PART // 2 * BLK
    shape = (half, rows, LANES)
    out_spec = pl.BlockSpec((1, rows, LANES), lambda d, r: (d, 0, 0))
    aliases = {}
    if shells is not None:
        rows = rows + shells.shape[1]
        shape = (half, 2, rows, LANES)
        args.append(shells)
        specs.append(pl.BlockSpec(shells.shape, lambda d, r: (0, 0, 0)))
        out_spec = pl.BlockSpec((1, 1, rows, LANES), lambda d, r: (d, int(far), 0, 0))
    if into is not None:
        aliases = {1 + len(args): 0}
        args.append(into)
        specs.append(pl.BlockSpec(memory_space=pl.ANY))
    return pl.pallas_call(
        functools.partial(pack_body, table, t, far, count, shells is not None),
        out_shape=jax.ShapeDtypeStruct(shape, BF16),
        grid_spec=pltpu.PrefetchScalarGridSpec(
            num_scalar_prefetch=1, grid=(half,), in_specs=specs, out_specs=out_spec
        ),
        input_output_aliases=aliases,
        compiler_params=pltpu.CompilerParams(vmem_limit_bytes=LIMIT),
        cost_estimate=SMALL,
        name="pack%d%s" % (t, "far" if far else "own"),
    )(tab, *args)


def fetch(table, t, ref, own, far, slots, sems):
    n = table.shape[1]
    half = n // 2
    a, g = table.column(ref), table.row(ref)
    for b in range(2):
        for c in range(2):
            source = table.x(ref, t, a, g * 2 + b, c)
            near = (source >= half) == (a >= half)
            index = jnp.where(source >= half, source - half, source)
            k = 2 * b + c

            @pl.when(near)
            def _():
                pltpu.make_async_copy(own(index), slots.at[k], sems.at[k]).start()

            @pl.when(jnp.logical_not(near))
            def _():
                start = 0
                for array in far(index):
                    piece = slots.at[k, start : start + array.shape[0]]
                    pltpu.make_async_copy(array, piece, sems.at[k]).start()
                    start += array.shape[0]


def await_slot(own, slots, sems, k):
    pltpu.make_async_copy(own(0), slots.at[k], sems.at[k]).wait()


def main_rows(p, q, put_first, put_second):
    low = lane_of((GROUP * BLK, LANES)) < 64

    def step(i, carry):
        row = i * GROUP
        rows = pl.ds(pl.multiple_of(row * BLK, GROUP * BLK), GROUP * BLK)
        u, v = p[rows, :].astype(F32), q[rows, :].astype(F32)
        x = row + lax.div(row, PART // 2) * (PART // 2)
        put_first(x, jnp.where(low, u, v).reshape(GROUP, BLK, LANES))
        second = pltpu.roll(jnp.where(low, v, u).astype(BF16), 64, 1)
        put_second(x + PART // 2, second.reshape(GROUP, BLK, LANES))
        return carry

    lax.fori_loop(0, 32 // GROUP, step, 0)


def pick_body(table, t, ref, own_ref, far_a, far_b, out, slots, sems):
    b = pl.program_id(0)
    own, far = lambda i: own_ref.at[i], lambda i: [far_a.at[i], far_b.at[i]]

    @pl.when(b == 0)
    def _():
        fetch(table, t, ref, own, far, slots, sems)

    await_slot(own, slots, sems, 2 * b)
    await_slot(own, slots, sems, 2 * b + 1)

    def put(x, value):
        out[pl.ds(x, GROUP)] = value.astype(BF16)

    main_rows(slots.at[2 * b], slots.at[2 * b + 1], put, put)


def pick(table, tab, t, own, far, shape):
    rows = own.shape[1]
    return pl.pallas_call(
        functools.partial(pick_body, table, t),
        out_shape=jax.ShapeDtypeStruct(shape, BF16),
        grid_spec=pltpu.PrefetchScalarGridSpec(
            num_scalar_prefetch=1,
            grid=(2,),
            in_specs=[pl.BlockSpec(memory_space=pl.ANY)] * 3,
            out_specs=pl.BlockSpec((64, BLK, LANES), lambda b, r: (0, b, 0)),
            scratch_shapes=[pltpu.VMEM((4, rows, LANES), BF16), pltpu.SemaphoreType.DMA((4,))],
        ),
        compiler_params=pltpu.CompilerParams(vmem_limit_bytes=LIMIT),
        cost_estimate=pl.CostEstimate(flops=2 * 64 * 128 * 128, bytes_accessed=4 << 20, transcendentals=0),
        name="pick",
    )(tab, own, *far)


XC = 16
SPAN = 6


def warp_body(table, t, ref, received, fixed, field, out, near, up, down, edge, turn, slots, sems):
    b, chunk = pl.program_id(0), pl.program_id(1)
    own, far = lambda i: received.at[i, 0], lambda i: [received.at[i, 1]]

    @pl.when((b == 0) & (chunk == 0))
    def _():
        fetch(table, t, ref, own, far, slots, sems)

    @pl.when(chunk == 0)
    def _():
        await_slot(own, slots, sems, 2 * b)
        await_slot(own, slots, sems, 2 * b + 1)
        p, q = slots.at[2 * b], slots.at[2 * b + 1]

        def put(x, value):
            near[pl.ds(x + 1, GROUP), 8:72, :] = value.astype(F32)

        main_rows(p, q, put, put)

        def both(start, size):
            u = p[start : start + size, :].astype(F32)
            v = q[start : start + size, :].astype(F32)
            mask = lane_of((size, LANES)) < 64
            return jnp.where(mask, u, pltpu.roll(v, 64, 1)), jnp.where(mask, pltpu.roll(u, 64, 1), v)

        first, second = both(MAIN, BLK)
        near[0, 8:72, :] = first
        near[65, 8:72, :] = second
        first, second = both(MAIN + 64, 80)
        edge[0] = first
        edge[1] = second

        a, g = table.column(ref), table.row(ref)
        z_p = table.z(ref, t, a, g * 2 + b, 0)
        z_q = table.z(ref, t, a, g * 2 + b, 1)
        row = lax.broadcasted_iota(jnp.int32, (128, 256), 0)
        col = lax.broadcasted_iota(jnp.int32, (128, 256), 1)
        inside = ((row == col + 1) & (col != 63)) | ((row == col - 129) & (col != 192))
        turn[0:128, :] = jnp.where(inside & ((col < 128) | (col > 128)), 1.0, 0.0).astype(BF16)
        turn[128:256, :] = jnp.where(col == jnp.where(z_p == 0, 63, 128), 1.0, 0.0).astype(BF16)
        turn[256:384, :] = jnp.where(col == jnp.where(z_q == 0, 127, 192), 1.0, 0.0).astype(BF16)
        face_p = p[MAIN + 144 : MAIN + 224, :].astype(F32)
        face_q = q[MAIN + 144 : MAIN + 224, :].astype(F32)
        lane = lane_of((80, LANES))

        def widen(j, carry):
            parts = []
            for k in range(SPAN):
                i = j * SPAN + k
                near[i, 7:8, :] = edge[0, pl.ds(i, 1), :]
                near[i, 72:73, :] = edge[1, pl.ds(i, 1), :]
                here = lane == i
                parts.append(
                    jnp.concatenate(
                        [
                            near[i].astype(BF16),
                            jnp.where(here, face_p, 0.0).astype(BF16),
                            jnp.where(here, face_q, 0.0).astype(BF16),
                        ],
                        axis=1,
                    )
                )
            got = jnp.dot(jnp.concatenate(parts, axis=0), turn[...], preferred_element_type=F32)
            got = got.reshape(SPAN, 80, 256)
            up[pl.ds(j * SPAN, SPAN)] = got[:, :, :LANES]
            down[pl.ds(j * SPAN, SPAN)] = got[:, :, LANES:]
            return carry

        lax.fori_loop(0, 66 // SPAN, widen, 0)

    def planes(j, carry):
        for tile in range(8):
            r = 8 * tile
            seen = {}

            def load(name, array, xi, ky):
                if (name, xi, ky) not in seen:
                    y0 = 7 + r + ky
                    seen[name, xi, ky] = array[chunk * XC + 4 * j + xi, y0 : y0 + 8, :]
                return seen[name, xi, ky]

            for xo in range(4):
                x = 4 * j + xo
                fx, fy, fz = field[0, x, r : r + 8, :], field[1, x, r : r + 8, :], field[2, x, r : r + 8, :]
                px, py, pz = fx > 0, fy > 0, fz > 0
                wx, wy, wz = jnp.abs(fx), jnp.abs(fy), jnp.abs(fz)
                per_x = []
                for kx in range(3):
                    per_y = []
                    for ky in range(3):
                        here = load("near", near, xo + kx, ky)
                        beside = jnp.where(pz, load("up", up, xo + kx, ky), load("down", down, xo + kx, ky))
                        per_y.append((here, beside))
                    aside = [jnp.where(py, per_y[2][i], per_y[0][i]) for i in range(2)]
                    per_x.append((per_y[1], aside))
                lines = []
                for s in range(2):
                    c00, c01, c10, c11 = [
                        per_x[1][v][i] if s == 0 else jnp.where(px, per_x[2][v][i], per_x[0][v][i])
                        for v in range(2)
                        for i in range(2)
                    ]
                    l0 = c00 + wz * (c01 - c00)
                    l1 = c10 + wz * (c11 - c10)
                    lines.append(l0 + wy * (l1 - l0))
                warped = lines[0] + wx * (lines[1] - lines[0])
                out[x, r : r + 8, :] = fixed[x, r : r + 8, :].astype(F32) - warped
        return carry

    lax.fori_loop(0, XC // 4, planes, 0)


def warp(table, tab, t, received, fixed, field):
    rows = received.shape[2]
    tile_x = fixed.shape[0]
    block = pl.BlockSpec((XC, BLK, LANES), lambda b, c, r: (c, b, 0))
    return pl.pallas_call(
        functools.partial(warp_body, table, t),
        out_shape=jax.ShapeDtypeStruct(fixed.shape, F32),
        grid_spec=pltpu.PrefetchScalarGridSpec(
            num_scalar_prefetch=1,
            grid=(2, tile_x // XC),
            in_specs=[
                pl.BlockSpec(memory_space=pl.ANY),
                block,
                pl.BlockSpec((3, XC, BLK, LANES), lambda b, c, r: (0, c, b, 0)),
            ],
            out_specs=block,
            scratch_shapes=[pltpu.VMEM((66, 80, LANES), F32)] * 3
            + [
                pltpu.VMEM((2, 80, LANES), F32),
                pltpu.VMEM((384, 256), BF16),
                pltpu.VMEM((4, rows, LANES), BF16),
                pltpu.SemaphoreType.DMA((4,)),
            ],
        ),
        compiler_params=pltpu.CompilerParams(vmem_limit_bytes=LIMIT),
        cost_estimate=pl.CostEstimate(flops=60 << 20, bytes_accessed=22 << 20, transcendentals=0),
        name="warp",
    )(tab, received, fixed, field)


def put_planes(is_warped, g, count, start, total, diff, value, value_y, fixed, fixed_y):
    def step(i, carry):
        f, v = fixed[i].astype(F32), value[i].astype(F32)
        fy, vy = fixed_y[i].astype(F32), value_y[i].astype(F32)
        fy = jnp.where(g == 1, fy[8:16], fy[0:8])
        if vy.shape[0] == 16:
            vy = jnp.where(g == 1, vy[8:16], vy[0:8])
        if is_warped:
            s, m, sy, my = f + v, f - v, fy + vy, fy - vy
        else:
            s, m, sy, my = 2.0 * f - v, v, 2.0 * fy - vy, vy
        zero = jnp.zeros_like(sy)
        j = start + i
        total[j, 16:144, :] = s
        diff[j, 16:144, :] = m
        total[j, 8:16, :] = jnp.where(g == 1, sy, zero)
        total[j, 144:152, :] = jnp.where(g == 0, sy, zero)
        diff[j, 8:16, :] = jnp.where(g == 1, my, zero)
        diff[j, 144:152, :] = jnp.where(g == 0, my, zero)
        return carry

    lax.fori_loop(0, count, step, 0)


def update_planes(g, count, base, start, total, diff, summed, prior, prior_y, source):
    lane = lane_of((8, LANES))

    def step(i, carry):
        j = start + i
        for t in range(18):
            r = 8 + 8 * t
            here = total[j, r : r + 8, :]
            gx = total[j + 1, r : r + 8, :] - total[j - 1, r : r + 8, :]
            gy = total[j, r + 1 : r + 9, :] - total[j, r - 1 : r + 7, :]
            gz = jnp.where(lane < LANES - 1, pltpu.roll(here, LANES - 1, 1), 0.0) - jnp.where(
                lane > 0, pltpu.roll(here, 1, 1), 0.0
            )
            m = diff[j, r : r + 8, :]
            size = (gx * gx + gy * gy) + (gz * gz + (16.0 * m * m + 16.0 * STIFF))
            inv = pl.reciprocal(size, approx=True)
            inv = inv * (2.0 - size * inv)
            scale = (4.0 * m) * inv
            for c, grad in enumerate((gx, gy, gz)):
                value = scale * grad
                if prior is not None:
                    if 1 <= t <= 16:
                        value = value + prior[c, source + i, 8 * t - 8 : 8 * t, :]
                    else:
                        own = (g == 1) if t == 0 else (g == 0)
                        value = value + jnp.where(own, prior_y[c, source + i, 0:8, :], 0.0)
                summed[c, base + i, r - 8 : r, :] = value
        return carry

    lax.fori_loop(0, count, step, 0)


def smooth_planes(before, after, summed, along, wide, weights, out):
    w = [float(v) for v in taps()]

    def tap_sum(values):
        acc = w[RADIUS] * values[RADIUS]
        for k in range(RADIUS):
            acc = acc + w[k] * (values[k] + values[2 * RADIUS - k])
        return acc

    def rows(t, carry):
        r = pl.ds(pl.multiple_of(8 * t, 8), 8)
        for c in range(3):
            planes = [summed[c, before + j, r, :] for j in range(CH)]
            planes += [summed[c, after + j, r, :] for j in range(CH)]
            for o in range(CH):
                along[c, o, r, :] = tap_sum(planes[o : o + 2 * RADIUS + 1])
        return carry

    lax.fori_loop(0, 18, rows, 0)

    def plane(o, carry):
        for c in range(3):
            for t in range(8):
                r = 16 * t + 4
                acc = tap_sum([along[c, o, r + k : r + k + 16, :] for k in range(2 * RADIUS + 1)])
                high = acc.astype(BF16)
                wide[c * 128 + 16 * t : c * 128 + 16 * t + 16, 0:LANES] = high
                wide[c * 128 + 16 * t : c * 128 + 16 * t + 16, LANES:] = (acc - high.astype(F32)).astype(BF16)
        got = jnp.dot(wide[...], weights[...], preferred_element_type=F32)
        for c in range(3):
            part = got[c * 128 : c * 128 + 128]
            out[c, o] = part[:, :LANES] + part[:, LANES:]
        return carry

    lax.fori_loop(0, CH, plane, 0)


def scratch(planes):
    return [
        pltpu.VMEM((planes, 160, LANES), F32),
        pltpu.VMEM((planes, 160, LANES), F32),
        pltpu.VMEM((3, 16, 144, LANES), F32),
        pltpu.VMEM((3, CH, 144, LANES), F32),
        pltpu.VMEM((384, 256), BF16),
    ]


def inner_body(table, is_warped, ref, weights, value, value_y, fixed, fixed_y, *refs):
    prior, prior_y = (None, None) if is_warped else refs[:2]
    out, total, diff, summed, along, wide = refs[0 if is_warped else 2 :]
    k = pl.program_id(0)
    g = table.row(ref)
    cur = lax.rem(k, 2) * CH
    put_planes(is_warped, g, CH + 2, 0, total, diff, value, value_y, fixed, fixed_y)
    update_planes(g, CH, cur, 1, total, diff, summed, prior, prior_y, 0)

    @pl.when(k > 0)
    def _():
        smooth_planes(CH - cur, cur, summed, along, wide, weights, out)


def inner(table, tab, weights, value, value_y, fixed, fixed_y, prior=None, prior_y=None):
    tile_x = fixed.shape[0]
    is_warped = prior is None

    def window(array, planes, first):
        dims = array.shape
        if len(dims) == 3:
            return pl.BlockSpec(
                (pl.Element(planes), pl.Element(dims[1]), pl.Element(dims[2])), lambda k, r: (k * CH + first, 0, 0)
            )
        return pl.BlockSpec(
            (pl.Element(dims[0]), pl.Element(planes), pl.Element(dims[2]), pl.Element(dims[3])),
            lambda k, r: (0, k * CH + first, 0, 0),
        )

    specs = [pl.BlockSpec(weights.shape, lambda k, r: (0, 0))]
    args = [weights]
    for array in (value, value_y, fixed, fixed_y):
        specs.append(window(array, CH + 2, 3))
        args.append(array)
    if not is_warped:
        for array in (prior, prior_y):
            specs.append(window(array, CH, 4))
            args.append(array)
    return pl.pallas_call(
        functools.partial(inner_body, table, is_warped),
        out_shape=jax.ShapeDtypeStruct((3,) + fixed.shape, F32),
        grid_spec=pltpu.PrefetchScalarGridSpec(
            num_scalar_prefetch=1,
            grid=(tile_x // CH - 1,),
            in_specs=specs,
            out_specs=pl.BlockSpec((3, CH) + fixed.shape[1:], lambda k, r: (0, jnp.maximum(k, 1), 0, 0)),
            scratch_shapes=scratch(CH + 2),
        ),
        compiler_params=pltpu.CompilerParams(vmem_limit_bytes=LIMIT),
        cost_estimate=pl.CostEstimate(flops=200 << 20, bytes_accessed=30 << 20, transcendentals=0),
        name="inner%d" % (not is_warped),
    )(tab, *args)


def rim_body(table, is_warped, ref, weights, value, value_y, fixed, fixed_y, *refs):
    halo = refs[:4]
    refs = refs[4:]
    if is_warped:
        prior = prior_y = None
    else:
        prior, prior_y, prior_low, prior_high = refs[:4]
        refs = refs[4:]
    _, out, total, diff, summed, along, wide = refs
    k = pl.program_id(0)
    g = table.row(ref)
    put_planes(is_warped, g, 13, 5 * (1 - k), total, diff, value, value_y, fixed, fixed_y)

    def side(at, value_x, fixed_x):
        v_main, v_y = value_x.at[:, :128, :], value_x.at[:, 128:, :]
        f_main, f_y = fixed_x.at[:, :128, :], fixed_x.at[:, 128:, :]
        put_planes(is_warped, g, 5, at, total, diff, v_main, v_y, f_main, f_y)

    @pl.when(k == 0)
    def _():
        side(0, halo[0], halo[2])

    @pl.when(k == 1)
    def _():
        side(13, halo[1], halo[3])

    if is_warped:
        update_planes(g, 16, 0, 1, total, diff, summed, None, None, 0)
    else:
        update_planes(g, 12, 4 * (1 - k), 1 + 4 * (1 - k), total, diff, summed, prior, prior_y, 0)

        def outside(at, prior_x):
            update_planes(
                g, 4, at, 1 + at, total, diff, summed, prior_x.at[:, :, :128, :], prior_x.at[:, :, 128:, :], 0
            )

        @pl.when(k == 0)
        def _():
            outside(0, prior_low)

        @pl.when(k == 1)
        def _():
            outside(12, prior_high)

    smooth_planes(0, CH, summed, along, wide, weights, out)


def rim(table, tab, weights, field, value, value_y, fixed, fixed_y, halo, prior=None, prior_y=None, prior_x=()):
    tile_x = fixed.shape[0]
    is_warped = prior is None

    def window(array, planes):
        dims = array.shape
        if len(dims) == 3:
            return pl.BlockSpec(
                (pl.Element(planes), pl.Element(dims[1]), pl.Element(dims[2])),
                lambda k, r: (k * (tile_x - planes), 0, 0),
            )
        return pl.BlockSpec(
            (pl.Element(dims[0]), pl.Element(planes), pl.Element(dims[2]), pl.Element(dims[3])),
            lambda k, r: (0, k * (tile_x - planes), 0, 0),
        )

    def whole(array):
        return pl.BlockSpec(array.shape, lambda k, r: (0,) * array.ndim)

    specs, args = [whole(weights)], [weights]
    for array in (value, value_y, fixed, fixed_y):
        specs.append(window(array, 13))
        args.append(array)
    for array in halo:
        specs.append(whole(array))
        args.append(array)
    if not is_warped:
        for array in (prior, prior_y):
            specs.append(window(array, 12))
            args.append(array)
        for array in prior_x:
            specs.append(whole(array))
            args.append(array)
    specs.append(pl.BlockSpec(memory_space=pl.ANY))
    args.append(field)
    last = tile_x // CH - 1
    return pl.pallas_call(
        functools.partial(rim_body, table, is_warped),
        out_shape=jax.ShapeDtypeStruct(field.shape, F32),
        grid_spec=pltpu.PrefetchScalarGridSpec(
            num_scalar_prefetch=1,
            grid=(2,),
            in_specs=specs,
            out_specs=pl.BlockSpec((3, CH) + fixed.shape[1:], lambda k, r: (0, k * last, 0, 0)),
            scratch_shapes=scratch(18),
        ),
        input_output_aliases={len(args): 0},
        compiler_params=pltpu.CompilerParams(vmem_limit_bytes=LIMIT),
        cost_estimate=pl.CostEstimate(flops=60 << 20, bytes_accessed=10 << 20, transcendentals=0),
        name="rim%d" % (not is_warped),
    )(tab, *args)


def swap_y(value, g, rows):
    length = value.shape[-2]
    first = lax.slice_in_dim(value, 0, rows, axis=value.ndim - 2)
    last = lax.slice_in_dim(value, length - rows, length, axis=value.ndim - 2)
    return lax.ppermute(jnp.where(g == 0, last, first), "gy", [(0, 1), (1, 0)])


def shift_x(value, value_y, width):
    size = lax.axis_size("gx")
    axis = value.ndim - 3
    length = value.shape[axis]
    up = [(i, i + 1) for i in range(size - 1)]
    down = [(j, i) for i, j in up]

    def part(start):
        return jnp.concatenate(
            [lax.slice_in_dim(v, start, start + width, axis=axis) for v in (value, value_y)], axis=value.ndim - 2
        )

    return lax.ppermute(part(length - width), "gx", up), lax.ppermute(part(0), "gx", down)


def column_body(table, ref, low, main, high, rows_y, out):
    g = table.row(ref)
    lane = lane_of((128, LANES))
    small = lane_of((16, LANES))

    def put(i, acc, plane, plane_y):
        shift = lax.rem(i + 256 - (BLK - 1), LANES)
        got = pltpu.roll(plane, shift, 1)
        got_y = pltpu.roll(plane_y, shift, 1)
        return (
            jnp.where(lane == i, got, acc[0]),
            jnp.where(lane == i + 1, got, acc[1]),
            jnp.where(small == i, got_y, acc[2]),
            jnp.where(small == i + 1, got_y, acc[3]),
        )

    acc = (jnp.zeros((128, LANES), F32),) * 2 + (jnp.zeros((16, LANES), F32),) * 2
    acc = put(0, acc, low[0].astype(F32), rows_y[0].astype(F32))
    acc = put(65, acc, high[0].astype(F32), rows_y[65].astype(F32))

    def step(x, acc):
        return put(x + 1, acc, main[x].astype(F32), rows_y[x + 1].astype(F32))

    acc = lax.fori_loop(0, 64, step, acc)
    for k in range(2):
        full, part = acc[k], acc[2 + k]
        if k:
            full, part = pltpu.roll(full, LANES - 1, 1), pltpu.roll(part, LANES - 1, 1)
        out[k, 16:144, :] = full.astype(BF16)
        out[k, 0:16, :] = jnp.where(g == 1, part, 0.0).astype(BF16)
        out[k, 144:160, :] = jnp.where(g == 0, part, 0.0).astype(BF16)


def columns(table, tab, low, main, high, rows_y):
    args = (low, main, high, rows_y)
    return pl.pallas_call(
        functools.partial(column_body, table),
        out_shape=jax.ShapeDtypeStruct((2, 160, LANES), BF16),
        grid_spec=pltpu.PrefetchScalarGridSpec(
            num_scalar_prefetch=1,
            grid=(1,),
            in_specs=[pl.BlockSpec(v.shape, lambda d, r: (0, 0, 0)) for v in args],
            out_specs=pl.BlockSpec((2, 160, LANES), lambda d, r: (0, 0, 0)),
        ),
        compiler_params=pltpu.CompilerParams(vmem_limit_bytes=LIMIT),
        cost_estimate=SMALL,
        name="columns",
    )(tab, *args)


def shell_rows(low, main, high, rows_y, column, g):
    def at(y):
        return jnp.concatenate([low[:, y], main[:, y], high[:, y]])

    below = [jnp.where(g == 1, rows_y[:, -1], 0), at(BLK - 1)]
    above = [at(BLK), jnp.where(g == 0, rows_y[:, 0], 0)]
    faces = []
    for b in range(2):
        y = slice(b * BLK, b * BLK + BLK)
        for c in range(2):
            z = slice(c * BLK, c * BLK + BLK)
            side_x = jnp.concatenate([low[0, y, z], high[0, y, z]], axis=1)
            side_y = jnp.concatenate([below[b][:, z], above[b][:, z]], axis=1)
            side_z = column[1 - c, b * BLK + 8 : b * BLK + 88]
            faces.append(jnp.concatenate([side_x, jnp.pad(side_y, ((0, 14), (0, 0))), side_z], axis=0))
    return jnp.stack(faces)


def local(fixed, moving, source_x, source_z):
    g = lax.axis_index("gy")
    table = Table(source_x.shape)
    tab = jnp.concatenate(
        [
            source_x.reshape(-1),
            source_z.reshape(-1),
            jnp.stack([lax.axis_index("gx"), g]).astype(jnp.int32),
        ]
    )
    weights = band()
    n = lax.axis_size("gx")
    half = n // 2
    opposite = [(i, (i + half) % n) for i in range(n)]
    halves = [list(range(half)), list(range(half, n))]

    def send(slots):
        return lax.all_to_all(slots, "gx", split_axis=0, concat_axis=0, axis_index_groups=halves, tiled=True)

    tile_x = fixed.shape[0]
    mirror_a = lax.ppermute(moving[:PART], "gx", opposite)
    up = [(i, i + 1) for i in range(n - 1)]
    low = lax.ppermute(moving[-1:], "gx", up)
    high = lax.ppermute(moving[:1], "gx", [(j, i) for i, j in up])
    rest, low, high = lax.optimization_barrier((moving[PART:], low, high))
    mirror_b = lax.ppermute(rest, "gx", opposite)
    own0 = send(pack(table, tab, 0, False, [moving]))
    rows_y = swap_y(jnp.concatenate([fixed, low, moving, high]), g, 16)
    fixed_y, moving_y = rows_y[:tile_x], rows_y[tile_x:]
    fixed_x = shift_x(fixed, fixed_y, 5)
    column = columns(table, tab, low, moving, high, moving_y)
    shells = shell_rows(low, moving, high, moving_y, column, g)
    shells_far = lax.ppermute(shells, "gx", opposite)
    slots1 = pack(table, tab, 1, False, [moving], shells)
    far0_a = send(pack(table, tab, 0, True, [mirror_a]))
    mirror_b, own0, far0_a, shells_far, slots1, fixed_x = lax.optimization_barrier(
        (mirror_b, own0, far0_a, shells_far, slots1, fixed_x)
    )

    far0_b = send(pack(table, tab, 0, True, [mirror_b]))
    slots1 = pack(table, tab, 1, True, [mirror_a, mirror_b], shells_far, slots1)
    far0_b, slots1 = lax.optimization_barrier((far0_b, slots1))
    slots1 = send(slots1)

    warped = pick(table, tab, 0, own0, (far0_a, far0_b), fixed.shape)
    warped_y = swap_y(warped, g, 16)
    warped_x = shift_x(warped, warped_y, 5)
    field = inner(table, tab, weights, warped, warped_y, fixed, fixed_y)
    field = rim(table, tab, weights, field, warped, warped_y, fixed, fixed_y, (*warped_x, *fixed_x))
    field_y = swap_y(field, g, 8)
    field_x = shift_x(field, field_y, 4)

    mismatch = warp(table, tab, 1, slots1, fixed, field)
    mismatch_y = swap_y(mismatch, g, 8)
    mismatch_x = shift_x(mismatch, mismatch_y, 5)
    last = inner(table, tab, weights, mismatch, mismatch_y, fixed, fixed_y, field, field_y)
    last = rim(
        table, tab, weights, last, mismatch, mismatch_y, fixed, fixed_y, (*mismatch_x, *fixed_x), field, field_y, field_x
    )
    return (last, mismatch)


def solution(mesh):
    return jax.shard_map(
        local,
        mesh=mesh,
        in_specs=(
            P(("groups", "gx"), "gy", None),
            P(("groups", "gx"), "gy", None),
            P("groups", None, None, None),
            P("groups", None, None, None),
        ),
        out_specs=(P(None, ("groups", "gx"), "gy", None), P(("groups", "gx"), "gy", None)),
        check_vma=False,
    )
```

```python
import functools

import jax
import jax.numpy as jnp
import numpy as np
from jax import lax
from jax.experimental import pallas as pl
from jax.experimental.pallas import tpu as pltpu
from jax.sharding import PartitionSpec as P

BLK = 64
RADIUS = 4
STIFF = 0.05
LANES = 128
CH = 8
LARGE = pl.CostEstimate(flops=1 << 27, bytes_accessed=1 << 27, transcendentals=0)
SMALL = pl.CostEstimate(flops=1 << 16, bytes_accessed=1 << 16, transcendentals=0)
LIMIT = 56 * 1024 * 1024
F32 = jnp.float32
BF16 = jnp.bfloat16


def taps():
    k = np.arange(-RADIUS, RADIUS + 1).astype(np.float32)
    w = np.exp(-k * k / np.float32(4.5)).astype(np.float32)
    return (w / np.sum(w)).astype(np.float32)


def band():
    w = taps()
    full = np.zeros((LANES, LANES), np.float32)
    for i in range(LANES):
        for k in range(-RADIUS, RADIUS + 1):
            if 0 <= i + k < LANES:
                full[i + k, i] = w[k + RADIUS]
    high = jnp.asarray(full).astype(BF16)
    low = (jnp.asarray(full) - high.astype(F32)).astype(BF16)
    row = jnp.concatenate([high, low], 1)
    return jnp.concatenate([row, row], 0)


def lane_of(shape):
    return lax.broadcasted_iota(jnp.int32, shape, len(shape) - 1)


class Table:
    def __init__(self, shape):
        self.shape = shape
        self.size = int(np.prod(shape))

    def at(self, t, d, b, c):
        _, n, yb, zb = self.shape
        return ((t * n + d) * yb + b) * zb + c

    def x(self, ref, t, d, b, c):
        return ref[self.at(t, d, b, c)]

    def z(self, ref, t, d, b, c):
        return ref[self.size + self.at(t, d, b, c)]

    def column(self, ref):
        return ref[2 * self.size]

    def row(self, ref):
        return ref[2 * self.size + 1]


def wanted_block(table, ref, t, d, column):
    g = table.row(ref)
    blk_y, blk_z, out_z = jnp.int32(0), jnp.int32(0), jnp.int32(0)
    for b in range(2):
        for c in range(2):
            hit = table.x(ref, t, d, g * 2 + b, c) == column
            blk_y = jnp.where(hit, b, blk_y)
            blk_z = jnp.where(hit, table.z(ref, t, d, g * 2 + b, c), blk_z)
            out_z = jnp.where(hit, c, out_z)
    return blk_y, blk_z, out_z


MAIN = 32 * BLK
GROUP = 8
PART = 32


def pack_body(table, t, far, count, shell, ref, *refs):
    n = table.shape[1]
    half = n // 2
    a = table.column(ref)
    here = (a >= half).astype(jnp.int32)
    column = a if not far else jnp.where(a >= half, a - half, a + half)
    blk_y, blk_z, out_z = wanted_block(table, ref, t, here * half + pl.program_id(0), column)
    parts, out = refs[:count], refs[-1]
    y0 = pl.multiple_of(blk_y * BLK, BLK)
    keep = (lane_of((GROUP, BLK, LANES)) < 64) == (blk_z == 0)
    turn = jnp.where(blk_z == out_z, 0, PART // 2)
    for k, mov in enumerate(parts):
        for x in range(0, PART // 2, GROUP):
            same = mov[pl.ds(x + turn, GROUP), pl.ds(y0, BLK), :]
            other = mov[pl.ds(x + PART // 2 - turn, GROUP), pl.ds(y0, BLK), :]
            other = pltpu.roll(other.reshape(GROUP * BLK, LANES), 64, 1).reshape(GROUP, BLK, LANES)
            got = jnp.where(keep, same.astype(F32), other.astype(F32)).astype(BF16)
            row = (k * PART // 2 + x) * BLK
            out[0, row : row + GROUP * BLK, :] = got.reshape(GROUP * BLK, LANES)
    if shell:
        out[0, MAIN:, :] = refs[count][blk_y * 2 + blk_z]


def pack(table, tab, t, far, parts, shells=None):
    half = table.shape[1] // 2
    args, specs = [], []
    for part in parts:
        for i in range(part.shape[0] // PART):
            args.append(part)
            specs.append(pl.BlockSpec((PART,) + part.shape[1:], lambda d, r, i=i: (i, 0, 0)))
    count = len(args)
    rows = count * PART // 2 * BLK
    if shells is not None:
        rows = rows + shells.shape[1]
        args.append(shells)
        specs.append(pl.BlockSpec(shells.shape, lambda d, r: (0, 0, 0)))
    return pl.pallas_call(
        functools.partial(pack_body, table, t, far, count, shells is not None),
        out_shape=jax.ShapeDtypeStruct((half, rows, LANES), BF16),
        grid_spec=pltpu.PrefetchScalarGridSpec(
            num_scalar_prefetch=1,
            grid=(half,),
            in_specs=specs,
            out_specs=pl.BlockSpec((1, rows, LANES), lambda d, r: (d, 0, 0)),
        ),
        compiler_params=pltpu.CompilerParams(vmem_limit_bytes=LIMIT),
        cost_estimate=LARGE if t == 1 and far else SMALL,
        name="pack%d%s" % (t, "far" if far else "own"),
    )(tab, *args)


def fetch(table, t, ref, own, far, slots, sems):
    n = table.shape[1]
    half = n // 2
    a, g = table.column(ref), table.row(ref)
    for b in range(2):
        for c in range(2):
            source = table.x(ref, t, a, g * 2 + b, c)
            near = (source >= half) == (a >= half)
            index = jnp.where(source >= half, source - half, source)
            k = 2 * b + c

            @pl.when(near)
            def _():
                pltpu.make_async_copy(own(index), slots.at[k], sems.at[k]).start()

            @pl.when(jnp.logical_not(near))
            def _():
                pltpu.make_async_copy(far(index), slots.at[k], sems.at[k]).start()


def await_slot(own, slots, sems, k):
    pltpu.make_async_copy(own(0), slots.at[k], sems.at[k]).wait()


def main_rows(p, q, put_first, put_second):
    low = lane_of((GROUP * BLK, LANES)) < 64

    def step(i, carry):
        row = i * GROUP
        rows = pl.ds(pl.multiple_of(row * BLK, GROUP * BLK), GROUP * BLK)
        u, v = p[rows, :].astype(F32), q[rows, :].astype(F32)
        x = row + lax.div(row, PART // 2) * (PART // 2)
        put_first(x, jnp.where(low, u, v).reshape(GROUP, BLK, LANES))
        second = pltpu.roll(jnp.where(low, v, u).astype(BF16), 64, 1)
        put_second(x + PART // 2, second.reshape(GROUP, BLK, LANES))
        return carry

    lax.fori_loop(0, 32 // GROUP, step, 0)


def pick_body(table, t, ref, own_ref, far_ref, out, slots, sems):
    b = pl.program_id(0)
    own, far = lambda i: own_ref.at[i], lambda i: far_ref.at[i]

    @pl.when(b == 0)
    def _():
        fetch(table, t, ref, own, far, slots, sems)

    await_slot(own, slots, sems, 2 * b)
    await_slot(own, slots, sems, 2 * b + 1)

    def put(x, value):
        out[pl.ds(x, GROUP)] = value.astype(BF16)

    main_rows(slots.at[2 * b], slots.at[2 * b + 1], put, put)


def pick(table, tab, t, own, far, shape):
    rows = own.shape[1]
    return pl.pallas_call(
        functools.partial(pick_body, table, t),
        out_shape=jax.ShapeDtypeStruct(shape, BF16),
        grid_spec=pltpu.PrefetchScalarGridSpec(
            num_scalar_prefetch=1,
            grid=(2,),
            in_specs=[pl.BlockSpec(memory_space=pl.ANY)] * 2,
            out_specs=pl.BlockSpec((64, BLK, LANES), lambda b, r: (0, b, 0)),
            scratch_shapes=[pltpu.VMEM((4, rows, LANES), BF16), pltpu.SemaphoreType.DMA((4,))],
        ),
        compiler_params=pltpu.CompilerParams(vmem_limit_bytes=LIMIT),
        cost_estimate=pl.CostEstimate(flops=2 * 64 * 128 * 128, bytes_accessed=4 << 20, transcendentals=0),
        name="pick",
    )(tab, own, far)


XC = 16
SPAN = 8


def warp_body(table, t, ref, own_ref, far_ref, fixed, field, out, near, up, down, edge, turn, slots, sems):
    b, chunk = pl.program_id(0), pl.program_id(1)
    own, far = lambda i: own_ref.at[i], lambda i: far_ref.at[i]

    @pl.when((b == 0) & (chunk == 0))
    def _():
        fetch(table, t, ref, own, far, slots, sems)

    def widen(first, count):
        face_p = slots[2 * b, MAIN + 144 : MAIN + 224, :].astype(F32)
        face_q = slots[2 * b + 1, MAIN + 144 : MAIN + 224, :].astype(F32)
        lane = lane_of((80, LANES))
        parts = []
        for k in range(count):
            i = first + k
            near[i, 7:8, :] = edge[0, pl.ds(i, 1), :]
            near[i, 72:73, :] = edge[1, pl.ds(i, 1), :]
            here = lane == i
            sides = [jnp.where(here, face, 0.0).astype(BF16) for face in (face_p, face_q)]
            parts.append(jnp.concatenate([near[i].astype(BF16)] + sides, axis=1))
        got = jnp.dot(jnp.concatenate(parts, axis=0), turn[...], preferred_element_type=F32)
        got = got.reshape(count, 80, 256)
        up[pl.ds(first, count)] = got[:, :, :LANES]
        down[pl.ds(first, count)] = got[:, :, LANES:]

    @pl.when(chunk == 0)
    def _():
        await_slot(own, slots, sems, 2 * b)
        await_slot(own, slots, sems, 2 * b + 1)
        p, q = slots.at[2 * b], slots.at[2 * b + 1]

        def put(x, value):
            near[pl.ds(x + 1, GROUP), 8:72, :] = value.astype(F32)

        main_rows(p, q, put, put)

        def both(start, size):
            u = p[start : start + size, :].astype(F32)
            v = q[start : start + size, :].astype(F32)
            mask = lane_of((size, LANES)) < 64
            return jnp.where(mask, u, pltpu.roll(v, 64, 1)), jnp.where(mask, pltpu.roll(u, 64, 1), v)

        first, second = both(MAIN, BLK)
        near[0, 8:72, :] = first
        near[65, 8:72, :] = second
        first, second = both(MAIN + 64, 80)
        edge[0] = first
        edge[1] = second

        a, g = table.column(ref), table.row(ref)
        z_p = table.z(ref, t, a, g * 2 + b, 0)
        z_q = table.z(ref, t, a, g * 2 + b, 1)
        row = lax.broadcasted_iota(jnp.int32, (128, 256), 0)
        col = lax.broadcasted_iota(jnp.int32, (128, 256), 1)
        inside = ((row == col + 1) & (col != 63)) | ((row == col - 129) & (col != 192))
        turn[0:128, :] = jnp.where(inside, 1.0, 0.0).astype(BF16)
        turn[128:256, :] = jnp.where(col == jnp.where(z_p == 0, 63, 128), 1.0, 0.0).astype(BF16)
        turn[256:384, :] = jnp.where(col == jnp.where(z_q == 0, 127, 192), 1.0, 0.0).astype(BF16)
        widen(0, 2)

    for start in range(0, XC, SPAN):
        widen(chunk * XC + 2 + start, SPAN)

    def planes(j, carry):
        for tile in range(8):
            r = 8 * tile
            seen = {}

            def load(name, array, xi, ky):
                if (name, xi, ky) not in seen:
                    y0 = 7 + r + ky
                    seen[name, xi, ky] = array[chunk * XC + 4 * j + xi, y0 : y0 + 8, :]
                return seen[name, xi, ky]

            for xo in range(4):
                x = 4 * j + xo
                fx, fy, fz = field[0, x, r : r + 8, :], field[1, x, r : r + 8, :], field[2, x, r : r + 8, :]
                px, py, pz = fx > 0, fy > 0, fz > 0
                wx, wy, wz = jnp.abs(fx), jnp.abs(fy), jnp.abs(fz)
                per_x = []
                for kx in range(3):
                    per_y = []
                    for ky in range(3):
                        here = load("near", near, xo + kx, ky)
                        beside = jnp.where(pz, load("up", up, xo + kx, ky), load("down", down, xo + kx, ky))
                        per_y.append((here, beside))
                    aside = [jnp.where(py, per_y[2][i], per_y[0][i]) for i in range(2)]
                    per_x.append((per_y[1], aside))
                lines = []
                for s in range(2):
                    c00, c01, c10, c11 = [
                        per_x[1][v][i] if s == 0 else jnp.where(px, per_x[2][v][i], per_x[0][v][i])
                        for v in range(2)
                        for i in range(2)
                    ]
                    l0 = c00 + wz * (c01 - c00)
                    l1 = c10 + wz * (c11 - c10)
                    lines.append(l0 + wy * (l1 - l0))
                warped = lines[0] + wx * (lines[1] - lines[0])
                out[x, r : r + 8, :] = fixed[x, r : r + 8, :].astype(F32) - warped
        return carry

    lax.fori_loop(0, XC // 4, planes, 0)


def warp(table, tab, t, own, far, fixed, field):
    rows = own.shape[1]
    tile_x = fixed.shape[0]
    block = pl.BlockSpec((XC, BLK, LANES), lambda b, c, r: (c, b, 0))
    return pl.pallas_call(
        functools.partial(warp_body, table, t),
        out_shape=jax.ShapeDtypeStruct(fixed.shape, F32),
        grid_spec=pltpu.PrefetchScalarGridSpec(
            num_scalar_prefetch=1,
            grid=(2, tile_x // XC),
            in_specs=[
                pl.BlockSpec(memory_space=pl.ANY),
                pl.BlockSpec(memory_space=pl.ANY),
                block,
                pl.BlockSpec((3, XC, BLK, LANES), lambda b, c, r: (0, c, b, 0)),
            ],
            out_specs=block,
            scratch_shapes=[pltpu.VMEM((66, 80, LANES), F32)] * 3
            + [
                pltpu.VMEM((2, 80, LANES), F32),
                pltpu.VMEM((384, 256), BF16),
                pltpu.VMEM((4, rows, LANES), BF16),
                pltpu.SemaphoreType.DMA((4,)),
            ],
        ),
        compiler_params=pltpu.CompilerParams(vmem_limit_bytes=LIMIT),
        cost_estimate=pl.CostEstimate(flops=60 << 20, bytes_accessed=22 << 20, transcendentals=0),
        name="warp",
    )(tab, own, far, fixed, field)


def put_planes(is_warped, g, count, start, total, diff, value, value_y, fixed, fixed_y):
    def step(i, carry):
        f, v = fixed[i].astype(F32), value[i].astype(F32)
        fy, vy = fixed_y[i].astype(F32), value_y[i].astype(F32)
        fy = jnp.where(g == 1, fy[8:16], fy[0:8])
        if vy.shape[0] == 16:
            vy = jnp.where(g == 1, vy[8:16], vy[0:8])
        if is_warped:
            s, m, sy, my = f + v, f - v, fy + vy, fy - vy
        else:
            s, m, sy, my = 2.0 * f - v, v, 2.0 * fy - vy, vy
        zero = jnp.zeros_like(sy)
        j = start + i
        total[j, 16:144, :] = s
        diff[j, 16:144, :] = m
        total[j, 8:16, :] = jnp.where(g == 1, sy, zero)
        total[j, 144:152, :] = jnp.where(g == 0, sy, zero)
        diff[j, 8:16, :] = jnp.where(g == 1, my, zero)
        diff[j, 144:152, :] = jnp.where(g == 0, my, zero)
        return carry

    lax.fori_loop(0, count, step, 0)


def update_planes(g, count, base, start, total, diff, summed, prior, prior_y, source):
    lane = lane_of((8, LANES))

    def step(i, carry):
        j = start + i
        for t in range(18):
            r = 8 + 8 * t
            here = total[j, r : r + 8, :]
            gx = total[j + 1, r : r + 8, :] - total[j - 1, r : r + 8, :]
            gy = total[j, r + 1 : r + 9, :] - total[j, r - 1 : r + 7, :]
            gz = jnp.where(lane < LANES - 1, pltpu.roll(here, LANES - 1, 1), 0.0) - jnp.where(
                lane > 0, pltpu.roll(here, 1, 1), 0.0
            )
            m = diff[j, r : r + 8, :]
            size = (gx * gx + gy * gy) + (gz * gz + (16.0 * m * m + 16.0 * STIFF))
            inv = pl.reciprocal(size, approx=True)
            inv = inv * (2.0 - size * inv)
            scale = (4.0 * m) * inv
            for c, grad in enumerate((gx, gy, gz)):
                value = scale * grad
                if prior is not None:
                    if 1 <= t <= 16:
                        value = value + prior[c, source + i, 8 * t - 8 : 8 * t, :]
                    else:
                        own = (g == 1) if t == 0 else (g == 0)
                        value = value + jnp.where(own, prior_y[c, source + i, 0:8, :], 0.0)
                summed[c, base + i, r - 8 : r, :] = value
        return carry

    lax.fori_loop(0, count, step, 0, unroll=4)


def smooth_planes(before, after, summed, along, wide, weights, out):
    w = [float(v) for v in taps()]

    def tap_sum(values):
        acc = w[RADIUS] * values[RADIUS]
        for k in range(RADIUS):
            acc = acc + w[k] * (values[k] + values[2 * RADIUS - k])
        return acc

    def rows(t, carry):
        r = pl.ds(pl.multiple_of(8 * t, 8), 8)
        for c in range(3):
            planes = [summed[c, before + j, r, :] for j in range(CH)]
            planes += [summed[c, after + j, r, :] for j in range(CH)]
            for o in range(CH):
                along[c, o, r, :] = tap_sum(planes[o : o + 2 * RADIUS + 1])
        return carry

    lax.fori_loop(0, 18, rows, 0, unroll=2)

    for o in range(CH):
        lhs = wide.at[o]
        for c in range(3):
            for t in range(8):
                r = 16 * t + 4
                acc = tap_sum([along[c, o, r + k : r + k + 16, :] for k in range(2 * RADIUS + 1)])
                high = acc.astype(BF16)
                lhs[c * 128 + 16 * t : c * 128 + 16 * t + 16, 0:LANES] = high
                lhs[c * 128 + 16 * t : c * 128 + 16 * t + 16, LANES:] = (acc - high.astype(F32)).astype(BF16)
        got = jnp.dot(lhs[...], weights[...], preferred_element_type=F32)
        for c in range(3):
            part = got[c * 128 : c * 128 + 128]
            out[c, o] = part[:, :LANES] + part[:, LANES:]


def scratch(planes):
    return [
        pltpu.VMEM((planes, 160, LANES), F32),
        pltpu.VMEM((planes, 160, LANES), F32),
        pltpu.VMEM((3, 16, 144, LANES), F32),
        pltpu.VMEM((3, CH, 144, LANES), F32),
        pltpu.VMEM((CH, 384, 256), BF16),
    ]


def inner_body(table, is_warped, ref, weights, value, value_y, fixed, fixed_y, *refs):
    prior, prior_y = (None, None) if is_warped else refs[:2]
    out, total, diff, summed, along, wide = refs[0 if is_warped else 2 :]
    k = pl.program_id(0)
    g = table.row(ref)
    cur = lax.rem(k, 2) * CH
    put_planes(is_warped, g, CH + 2, 0, total, diff, value, value_y, fixed, fixed_y)
    update_planes(g, CH, cur, 1, total, diff, summed, prior, prior_y, 0)

    @pl.when(k > 0)
    def _():
        smooth_planes(CH - cur, cur, summed, along, wide, weights, out)


def inner(table, tab, weights, value, value_y, fixed, fixed_y, prior=None, prior_y=None):
    tile_x = fixed.shape[0]
    is_warped = prior is None

    def window(array, planes, first):
        dims = array.shape
        if len(dims) == 3:
            return pl.BlockSpec(
                (pl.Element(planes), pl.Element(dims[1]), pl.Element(dims[2])), lambda k, r: (k * CH + first, 0, 0)
            )
        return pl.BlockSpec(
            (pl.Element(dims[0]), pl.Element(planes), pl.Element(dims[2]), pl.Element(dims[3])),
            lambda k, r: (0, k * CH + first, 0, 0),
        )

    specs = [pl.BlockSpec(weights.shape, lambda k, r: (0, 0))]
    args = [weights]
    for array in (value, value_y, fixed, fixed_y):
        specs.append(window(array, CH + 2, 3))
        args.append(array)
    if not is_warped:
        for array in (prior, prior_y):
            specs.append(window(array, CH, 4))
            args.append(array)
    return pl.pallas_call(
        functools.partial(inner_body, table, is_warped),
        out_shape=jax.ShapeDtypeStruct((3,) + fixed.shape, F32),
        grid_spec=pltpu.PrefetchScalarGridSpec(
            num_scalar_prefetch=1,
            grid=(tile_x // CH - 1,),
            in_specs=specs,
            out_specs=pl.BlockSpec((3, CH) + fixed.shape[1:], lambda k, r: (0, jnp.maximum(k, 1), 0, 0)),
            scratch_shapes=scratch(CH + 2),
        ),
        compiler_params=pltpu.CompilerParams(vmem_limit_bytes=LIMIT),
        cost_estimate=pl.CostEstimate(flops=200 << 20, bytes_accessed=30 << 20, transcendentals=0),
        name="inner%d" % (not is_warped),
    )(tab, *args)


def rim_body(table, is_warped, ref, weights, value, value_y, fixed, fixed_y, *refs):
    halo = refs[:4]
    refs = refs[4:]
    if is_warped:
        prior = prior_y = None
    else:
        prior, prior_y, prior_low, prior_high = refs[:4]
        refs = refs[4:]
    _, out, total, diff, summed, along, wide = refs
    k = pl.program_id(0)
    g = table.row(ref)
    put_planes(is_warped, g, 13, 5 * (1 - k), total, diff, value, value_y, fixed, fixed_y)

    def side(at, value_x, fixed_x):
        v_main, v_y = value_x.at[:, :128, :], value_x.at[:, 128:, :]
        f_main, f_y = fixed_x.at[:, :128, :], fixed_x.at[:, 128:, :]
        put_planes(is_warped, g, 5, at, total, diff, v_main, v_y, f_main, f_y)

    @pl.when(k == 0)
    def _():
        side(0, halo[0], halo[2])

    @pl.when(k == 1)
    def _():
        side(13, halo[1], halo[3])

    if is_warped:
        update_planes(g, 16, 0, 1, total, diff, summed, None, None, 0)
    else:
        update_planes(g, 12, 4 * (1 - k), 1 + 4 * (1 - k), total, diff, summed, prior, prior_y, 0)

        def outside(at, prior_x):
            update_planes(
                g, 4, at, 1 + at, total, diff, summed, prior_x.at[:, :, :128, :], prior_x.at[:, :, 128:, :], 0
            )

        @pl.when(k == 0)
        def _():
            outside(0, prior_low)

        @pl.when(k == 1)
        def _():
            outside(12, prior_high)

    smooth_planes(0, CH, summed, along, wide, weights, out)


def rim(table, tab, weights, field, value, value_y, fixed, fixed_y, halo, prior=None, prior_y=None, prior_x=()):
    tile_x = fixed.shape[0]
    is_warped = prior is None

    def window(array, planes):
        dims = array.shape
        if len(dims) == 3:
            return pl.BlockSpec(
                (pl.Element(planes), pl.Element(dims[1]), pl.Element(dims[2])),
                lambda k, r: (k * (tile_x - planes), 0, 0),
            )
        return pl.BlockSpec(
            (pl.Element(dims[0]), pl.Element(planes), pl.Element(dims[2]), pl.Element(dims[3])),
            lambda k, r: (0, k * (tile_x - planes), 0, 0),
        )

    def whole(array):
        return pl.BlockSpec(array.shape, lambda k, r: (0,) * array.ndim)

    specs, args = [whole(weights)], [weights]
    for array in (value, value_y, fixed, fixed_y):
        specs.append(window(array, 13))
        args.append(array)
    for array in halo:
        specs.append(whole(array))
        args.append(array)
    if not is_warped:
        for array in (prior, prior_y):
            specs.append(window(array, 12))
            args.append(array)
        for array in prior_x:
            specs.append(whole(array))
            args.append(array)
    specs.append(pl.BlockSpec(memory_space=pl.ANY))
    args.append(field)
    last = tile_x // CH - 1
    return pl.pallas_call(
        functools.partial(rim_body, table, is_warped),
        out_shape=jax.ShapeDtypeStruct(field.shape, F32),
        grid_spec=pltpu.PrefetchScalarGridSpec(
            num_scalar_prefetch=1,
            grid=(2,),
            in_specs=specs,
            out_specs=pl.BlockSpec((3, CH) + fixed.shape[1:], lambda k, r: (0, k * last, 0, 0)),
            scratch_shapes=scratch(18),
        ),
        input_output_aliases={len(args): 0},
        compiler_params=pltpu.CompilerParams(vmem_limit_bytes=LIMIT),
        cost_estimate=pl.CostEstimate(flops=60 << 20, bytes_accessed=10 << 20, transcendentals=0),
        name="rim%d" % (not is_warped),
    )(tab, *args)


def swap_y(values, g, rows):
    def edge(value):
        axis, length = value.ndim - 2, value.shape[-2]
        first = lax.slice_in_dim(value, 0, rows, axis=axis)
        last = lax.slice_in_dim(value, length - rows, length, axis=axis)
        return jnp.where(g == 0, last, first)

    edges = [edge(value) for value in values]
    return lax.ppermute(jnp.concatenate(edges) if len(edges) > 1 else edges[0], "gy", [(0, 1), (1, 0)])


def shift_x(value, value_y, width):
    size = lax.axis_size("gx")
    axis = value.ndim - 3
    length = value.shape[axis]
    up = [(i, i + 1) for i in range(size - 1)]
    down = [(j, i) for i, j in up]

    def part(start):
        return jnp.concatenate(
            [lax.slice_in_dim(v, start, start + width, axis=axis) for v in (value, value_y)], axis=value.ndim - 2
        )

    return lax.ppermute(part(length - width), "gx", up), lax.ppermute(part(0), "gx", down)


def column_body(table, ref, low, main, high, rows_y, out):
    g = table.row(ref)
    lane = lane_of((128, LANES))
    small = lane_of((16, LANES))

    def put(i, acc, plane, plane_y):
        shift = lax.rem(i + 256 - (BLK - 1), LANES)
        got = pltpu.roll(plane, shift, 1)
        got_y = pltpu.roll(plane_y, shift, 1)
        return (
            jnp.where(lane == i, got, acc[0]),
            jnp.where(lane == i + 1, got, acc[1]),
            jnp.where(small == i, got_y, acc[2]),
            jnp.where(small == i + 1, got_y, acc[3]),
        )

    acc = (jnp.zeros((128, LANES), F32),) * 2 + (jnp.zeros((16, LANES), F32),) * 2
    acc = put(0, acc, low[0].astype(F32), rows_y[0].astype(F32))
    acc = put(65, acc, high[0].astype(F32), rows_y[65].astype(F32))

    def step(x, acc):
        return put(x + 1, acc, main[x].astype(F32), rows_y[x + 1].astype(F32))

    acc = lax.fori_loop(0, 64, step, acc)
    for k in range(2):
        full, part = acc[k], acc[2 + k]
        if k:
            full, part = pltpu.roll(full, LANES - 1, 1), pltpu.roll(part, LANES - 1, 1)
        out[k, 16:144, :] = full.astype(BF16)
        out[k, 0:16, :] = jnp.where(g == 1, part, 0.0).astype(BF16)
        out[k, 144:160, :] = jnp.where(g == 0, part, 0.0).astype(BF16)


def columns(table, tab, low, main, high, rows_y):
    args = (low, main, high, rows_y)
    return pl.pallas_call(
        functools.partial(column_body, table),
        out_shape=jax.ShapeDtypeStruct((2, 160, LANES), BF16),
        grid_spec=pltpu.PrefetchScalarGridSpec(
            num_scalar_prefetch=1,
            grid=(1,),
            in_specs=[pl.BlockSpec(v.shape, lambda d, r: (0, 0, 0)) for v in args],
            out_specs=pl.BlockSpec((2, 160, LANES), lambda d, r: (0, 0, 0)),
        ),
        compiler_params=pltpu.CompilerParams(vmem_limit_bytes=LIMIT),
        cost_estimate=SMALL,
        name="columns",
    )(tab, *args)


def shell_rows(low, main, high, rows_y, column, g):
    def at(y):
        return jnp.concatenate([low[:, y], main[:, y], high[:, y]])

    below = [jnp.where(g == 1, rows_y[:, -1], 0), at(BLK - 1)]
    above = [at(BLK), jnp.where(g == 0, rows_y[:, 0], 0)]
    faces = []
    for b in range(2):
        y = slice(b * BLK, b * BLK + BLK)
        for c in range(2):
            z = slice(c * BLK, c * BLK + BLK)
            side_x = jnp.concatenate([low[0, y, z], high[0, y, z]], axis=1)
            side_y = jnp.concatenate([below[b][:, z], above[b][:, z]], axis=1)
            side_z = column[1 - c, b * BLK + 8 : b * BLK + 88]
            faces.append(jnp.concatenate([side_x, jnp.pad(side_y, ((0, 14), (0, 0))), side_z], axis=0))
    return jnp.stack(faces)


def local(fixed, moving, source_x, source_z):
    g = lax.axis_index("gy")
    table = Table(source_x.shape)
    tab = jnp.concatenate(
        [
            source_x.reshape(-1),
            source_z.reshape(-1),
            jnp.stack([lax.axis_index("gx"), g]).astype(jnp.int32),
        ]
    )
    weights = band()
    n = lax.axis_size("gx")
    half = n // 2
    opposite = [(i, (i + half) % n) for i in range(n)]
    halves = [list(range(half)), list(range(half, n))]

    def send(slots):
        return lax.all_to_all(slots, "gx", split_axis=0, concat_axis=0, axis_index_groups=halves, tiled=True)

    tile_x = fixed.shape[0]
    hold = lax.optimization_barrier
    up = [(i, i + 1) for i in range(n - 1)]
    low = lax.ppermute(moving[-1:], "gx", up)
    high = lax.ppermute(moving[:1], "gx", [(j, i) for i, j in up])
    rows_y = swap_y([fixed, moving], g, 16)
    own0 = pack(table, tab, 0, False, [moving])
    first, low, high, rows_y, own0 = hold((moving, low, high, rows_y, own0))

    mirror_a = lax.ppermute(first[:PART], "gx", opposite)
    own0 = send(own0)
    rows_x = swap_y([low, high], g, 16)
    fixed_y = rows_y[:tile_x]
    moving_y = jnp.concatenate([rows_x[:1], rows_y[tile_x:], rows_x[1:]])
    column = columns(table, tab, low, moving, high, moving_y)
    shells = shell_rows(low, moving, high, moving_y, column, g)
    own1 = pack(table, tab, 1, False, [moving], shells)
    mirror_a, own0, own1, shells, rest = hold((mirror_a, own0, own1, shells, first[PART:]))

    mirror_b = lax.ppermute(rest, "gx", opposite)
    shells_far = lax.ppermute(shells, "gx", opposite)
    own1 = send(own1)
    fixed_x = shift_x(fixed, fixed_y, 5)
    mirror_b, shells_far, own1 = hold((mirror_b, shells_far, own1))

    far0 = send(pack(table, tab, 0, True, [mirror_a, mirror_b]))
    far1 = pack(table, tab, 1, True, [mirror_a, mirror_b], shells_far)
    _, far1 = hold((far0, far1))
    far1 = send(far1)

    warped = pick(table, tab, 0, own0, far0, fixed.shape)
    warped_y = swap_y([warped], g, 16)
    warped_x = shift_x(warped, warped_y, 5)
    field = inner(table, tab, weights, warped, warped_y, fixed, fixed_y)
    field = rim(table, tab, weights, field, warped, warped_y, fixed, fixed_y, (*warped_x, *fixed_x))
    field_y = swap_y([field], g, 8)
    field_x = shift_x(field, field_y, 4)

    mismatch = warp(table, tab, 1, own1, far1, fixed, field)
    mismatch_y = swap_y([mismatch], g, 8)
    mismatch_x = shift_x(mismatch, mismatch_y, 5)
    last = inner(table, tab, weights, mismatch, mismatch_y, fixed, fixed_y, field, field_y)
    last = rim(
        table, tab, weights, last, mismatch, mismatch_y, fixed, fixed_y, (*mismatch_x, *fixed_x), field, field_y, field_x
    )
    return (last, mismatch)


def solution(mesh):
    return jax.shard_map(
        local,
        mesh=mesh,
        in_specs=(
            P(("groups", "gx"), "gy", None),
            P(("groups", "gx"), "gy", None),
            P("groups", None, None, None),
            P("groups", None, None, None),
        ),
        out_specs=(P(None, ("groups", "gx"), "gy", None), P(("groups", "gx"), "gy", None)),
        check_vma=False,
    )
```

```python
import functools

import jax
import jax.numpy as jnp
import numpy as np
from jax import lax
from jax.experimental import pallas as pl
from jax.experimental.pallas import tpu as pltpu
from jax.sharding import PartitionSpec as P

BLK = 64
RADIUS = 4
STIFF = 0.05
LANES = 128
CH = 8
LARGE = pl.CostEstimate(flops=1 << 27, bytes_accessed=1 << 27, transcendentals=0)
SMALL = pl.CostEstimate(flops=1 << 16, bytes_accessed=1 << 16, transcendentals=0)
LIMIT = 56 * 1024 * 1024
F32 = jnp.float32
BF16 = jnp.bfloat16


def taps():
    k = np.arange(-RADIUS, RADIUS + 1).astype(np.float32)
    w = np.exp(-k * k / np.float32(4.5)).astype(np.float32)
    return (w / np.sum(w)).astype(np.float32)


def band():
    w = taps()
    full = np.zeros((LANES, LANES), np.float32)
    for i in range(LANES):
        for k in range(-RADIUS, RADIUS + 1):
            if 0 <= i + k < LANES:
                full[i + k, i] = w[k + RADIUS]
    high = jnp.asarray(full).astype(BF16)
    low = (jnp.asarray(full) - high.astype(F32)).astype(BF16)
    row = jnp.concatenate([high, low], 1)
    return jnp.concatenate([row, row], 0)


def lane_of(shape):
    return lax.broadcasted_iota(jnp.int32, shape, len(shape) - 1)


class Table:
    def __init__(self, shape):
        self.shape = shape
        self.size = int(np.prod(shape))

    def at(self, t, d, b, c):
        _, n, yb, zb = self.shape
        return ((t * n + d) * yb + b) * zb + c

    def x(self, ref, t, d, b, c):
        return ref[self.at(t, d, b, c)]

    def z(self, ref, t, d, b, c):
        return ref[self.size + self.at(t, d, b, c)]

    def column(self, ref):
        return ref[2 * self.size]

    def row(self, ref):
        return ref[2 * self.size + 1]


def wanted_block(table, ref, t, d, column):
    g = table.row(ref)
    blk_y, blk_z, out_z = jnp.int32(0), jnp.int32(0), jnp.int32(0)
    for b in range(2):
        for c in range(2):
            hit = table.x(ref, t, d, g * 2 + b, c) == column
            blk_y = jnp.where(hit, b, blk_y)
            blk_z = jnp.where(hit, table.z(ref, t, d, g * 2 + b, c), blk_z)
            out_z = jnp.where(hit, c, out_z)
    return blk_y, blk_z, out_z


MAIN = 32 * BLK
GROUP = 8
PART = 32


def pack_body(table, t, far, count, shell, ref, *refs):
    n = table.shape[1]
    half = n // 2
    a = table.column(ref)
    here = (a >= half).astype(jnp.int32)
    column = a if not far else jnp.where(a >= half, a - half, a + half)
    blk_y, blk_z, out_z = wanted_block(table, ref, t, here * half + pl.program_id(0), column)
    parts, out = refs[:count], refs[-1]
    y0 = pl.multiple_of(blk_y * BLK, BLK)
    keep = (lane_of((GROUP, BLK, LANES)) < 64) == (blk_z == 0)
    turn = jnp.where(blk_z == out_z, 0, PART // 2)
    for k, mov in enumerate(parts):
        for x in range(0, PART // 2, GROUP):
            same = mov[pl.ds(x + turn, GROUP), pl.ds(y0, BLK), :]
            other = mov[pl.ds(x + PART // 2 - turn, GROUP), pl.ds(y0, BLK), :]
            other = pltpu.roll(other.reshape(GROUP * BLK, LANES), 64, 1).reshape(GROUP, BLK, LANES)
            got = jnp.where(keep, same.astype(F32), other.astype(F32)).astype(BF16)
            row = (k * PART // 2 + x) * BLK
            out[0, row : row + GROUP * BLK, :] = got.reshape(GROUP * BLK, LANES)
    if shell:
        out[0, MAIN:, :] = refs[count][blk_y * 2 + blk_z]


def pack(table, tab, t, far, parts, shells=None):
    half = table.shape[1] // 2
    args, specs = [], []
    for part in parts:
        for i in range(part.shape[0] // PART):
            args.append(part)
            specs.append(pl.BlockSpec((PART,) + part.shape[1:], lambda d, r, i=i: (i, 0, 0)))
    count = len(args)
    rows = count * PART // 2 * BLK
    if shells is not None:
        rows = rows + shells.shape[1]
        args.append(shells)
        specs.append(pl.BlockSpec(shells.shape, lambda d, r: (0, 0, 0)))
    return pl.pallas_call(
        functools.partial(pack_body, table, t, far, count, shells is not None),
        out_shape=jax.ShapeDtypeStruct((half, rows, LANES), BF16),
        grid_spec=pltpu.PrefetchScalarGridSpec(
            num_scalar_prefetch=1,
            grid=(half,),
            in_specs=specs,
            out_specs=pl.BlockSpec((1, rows, LANES), lambda d, r: (d, 0, 0)),
        ),
        compiler_params=pltpu.CompilerParams(vmem_limit_bytes=LIMIT),
        cost_estimate=LARGE if t == 1 and far else SMALL,
        name="pack%d%s" % (t, "far" if far else "own"),
    )(tab, *args)


def fetch(table, t, ref, own, far, slots, sems):
    n = table.shape[1]
    half = n // 2
    a, g = table.column(ref), table.row(ref)
    for b in range(2):
        for c in range(2):
            source = table.x(ref, t, a, g * 2 + b, c)
            near = (source >= half) == (a >= half)
            index = jnp.where(source >= half, source - half, source)
            k = 2 * b + c

            @pl.when(near)
            def _():
                pltpu.make_async_copy(own(index), slots.at[k], sems.at[k]).start()

            @pl.when(jnp.logical_not(near))
            def _():
                pltpu.make_async_copy(far(index), slots.at[k], sems.at[k]).start()


def await_slot(own, slots, sems, k):
    pltpu.make_async_copy(own(0), slots.at[k], sems.at[k]).wait()


def main_rows(p, q, put_first, put_second):
    low = lane_of((GROUP * BLK, LANES)) < 64

    def step(i, carry):
        row = i * GROUP
        rows = pl.ds(pl.multiple_of(row * BLK, GROUP * BLK), GROUP * BLK)
        u, v = p[rows, :].astype(F32), q[rows, :].astype(F32)
        x = row + lax.div(row, PART // 2) * (PART // 2)
        put_first(x, jnp.where(low, u, v).reshape(GROUP, BLK, LANES))
        second = pltpu.roll(jnp.where(low, v, u).astype(BF16), 64, 1)
        put_second(x + PART // 2, second.reshape(GROUP, BLK, LANES))
        return carry

    lax.fori_loop(0, 32 // GROUP, step, 0)


def pick_body(table, t, ref, own_ref, far_ref, out, slots, sems):
    b = pl.program_id(0)
    own, far = lambda i: own_ref.at[i], lambda i: far_ref.at[i]

    @pl.when(b == 0)
    def _():
        fetch(table, t, ref, own, far, slots, sems)

    await_slot(own, slots, sems, 2 * b)
    await_slot(own, slots, sems, 2 * b + 1)

    def put(x, value):
        out[pl.ds(x, GROUP)] = value.astype(BF16)

    main_rows(slots.at[2 * b], slots.at[2 * b + 1], put, put)


def pick(table, tab, t, own, far, shape):
    rows = own.shape[1]
    return pl.pallas_call(
        functools.partial(pick_body, table, t),
        out_shape=jax.ShapeDtypeStruct(shape, BF16),
        grid_spec=pltpu.PrefetchScalarGridSpec(
            num_scalar_prefetch=1,
            grid=(2,),
            in_specs=[pl.BlockSpec(memory_space=pl.ANY)] * 2,
            out_specs=pl.BlockSpec((64, BLK, LANES), lambda b, r: (0, b, 0)),
            scratch_shapes=[pltpu.VMEM((4, rows, LANES), BF16), pltpu.SemaphoreType.DMA((4,))],
        ),
        compiler_params=pltpu.CompilerParams(vmem_limit_bytes=LIMIT),
        cost_estimate=pl.CostEstimate(flops=2 * 64 * 128 * 128, bytes_accessed=4 << 20, transcendentals=0),
        name="pick",
    )(tab, own, far)


XC = 16
SPAN = 8


def warp_body(table, t, ref, own_ref, far_ref, fixed, field, out, near, up, down, edge, turn, slots, sems):
    b, chunk = pl.program_id(0), pl.program_id(1)
    own, far = lambda i: own_ref.at[i], lambda i: far_ref.at[i]

    @pl.when((b == 0) & (chunk == 0))
    def _():
        fetch(table, t, ref, own, far, slots, sems)

    def widen(first, count):
        face_p = slots[2 * b, MAIN + 144 : MAIN + 224, :].astype(F32)
        face_q = slots[2 * b + 1, MAIN + 144 : MAIN + 224, :].astype(F32)
        lane = lane_of((80, LANES))
        parts = []
        for k in range(count):
            i = first + k
            near[i, 7:8, :] = edge[0, pl.ds(i, 1), :]
            near[i, 72:73, :] = edge[1, pl.ds(i, 1), :]
            here = lane == i
            sides = [jnp.where(here, face, 0.0).astype(BF16) for face in (face_p, face_q)]
            parts.append(jnp.concatenate([near[i].astype(BF16)] + sides, axis=1))
        got = jnp.dot(jnp.concatenate(parts, axis=0), turn[...], preferred_element_type=F32)
        got = got.reshape(count, 80, 256)
        up[pl.ds(first, count)] = got[:, :, :LANES]
        down[pl.ds(first, count)] = got[:, :, LANES:]

    @pl.when(chunk == 0)
    def _():
        await_slot(own, slots, sems, 2 * b)
        await_slot(own, slots, sems, 2 * b + 1)
        p, q = slots.at[2 * b], slots.at[2 * b + 1]

        def put(x, value):
            near[pl.ds(x + 1, GROUP), 8:72, :] = value.astype(F32)

        main_rows(p, q, put, put)

        def both(start, size):
            u = p[start : start + size, :].astype(F32)
            v = q[start : start + size, :].astype(F32)
            mask = lane_of((size, LANES)) < 64
            return jnp.where(mask, u, pltpu.roll(v, 64, 1)), jnp.where(mask, pltpu.roll(u, 64, 1), v)

        first, second = both(MAIN, BLK)
        near[0, 8:72, :] = first
        near[65, 8:72, :] = second
        first, second = both(MAIN + 64, 80)
        edge[0] = first
        edge[1] = second

        a, g = table.column(ref), table.row(ref)
        z_p = table.z(ref, t, a, g * 2 + b, 0)
        z_q = table.z(ref, t, a, g * 2 + b, 1)
        row = lax.broadcasted_iota(jnp.int32, (128, 256), 0)
        col = lax.broadcasted_iota(jnp.int32, (128, 256), 1)
        inside = ((row == col + 1) & (col != 63)) | ((row == col - 129) & (col != 192))
        turn[0:128, :] = jnp.where(inside, 1.0, 0.0).astype(BF16)
        turn[128:256, :] = jnp.where(col == jnp.where(z_p == 0, 63, 128), 1.0, 0.0).astype(BF16)
        turn[256:384, :] = jnp.where(col == jnp.where(z_q == 0, 127, 192), 1.0, 0.0).astype(BF16)
        widen(0, 2)

    for start in range(0, XC, SPAN):
        widen(chunk * XC + 2 + start, SPAN)

    def planes(j, carry):
        for tile in range(8):
            r = 8 * tile
            seen = {}

            def load(name, array, xi, ky):
                if (name, xi, ky) not in seen:
                    y0 = 7 + r + ky
                    seen[name, xi, ky] = array[chunk * XC + 4 * j + xi, y0 : y0 + 8, :]
                return seen[name, xi, ky]

            for xo in range(4):
                x = 4 * j + xo
                fx, fy, fz = field[0, x, r : r + 8, :], field[1, x, r : r + 8, :], field[2, x, r : r + 8, :]
                px, py, pz = fx > 0, fy > 0, fz > 0
                wx, wy, wz = jnp.abs(fx), jnp.abs(fy), jnp.abs(fz)
                per_x = []
                for kx in range(3):
                    per_y = []
                    for ky in range(3):
                        here = load("near", near, xo + kx, ky)
                        beside = jnp.where(pz, load("up", up, xo + kx, ky), load("down", down, xo + kx, ky))
                        per_y.append((here, beside))
                    aside = [jnp.where(py, per_y[2][i], per_y[0][i]) for i in range(2)]
                    per_x.append((per_y[1], aside))
                lines = []
                for s in range(2):
                    c00, c01, c10, c11 = [
                        per_x[1][v][i] if s == 0 else jnp.where(px, per_x[2][v][i], per_x[0][v][i])
                        for v in range(2)
                        for i in range(2)
                    ]
                    l0 = c00 + wz * (c01 - c00)
                    l1 = c10 + wz * (c11 - c10)
                    lines.append(l0 + wy * (l1 - l0))
                warped = lines[0] + wx * (lines[1] - lines[0])
                out[x, r : r + 8, :] = fixed[x, r : r + 8, :].astype(F32) - warped
        return carry

    lax.fori_loop(0, XC // 4, planes, 0)


def warp(table, tab, t, own, far, fixed, field):
    rows = own.shape[1]
    tile_x = fixed.shape[0]
    block = pl.BlockSpec((XC, BLK, LANES), lambda b, c, r: (c, b, 0))
    return pl.pallas_call(
        functools.partial(warp_body, table, t),
        out_shape=jax.ShapeDtypeStruct(fixed.shape, F32),
        grid_spec=pltpu.PrefetchScalarGridSpec(
            num_scalar_prefetch=1,
            grid=(2, tile_x // XC),
            in_specs=[
                pl.BlockSpec(memory_space=pl.ANY),
                pl.BlockSpec(memory_space=pl.ANY),
                block,
                pl.BlockSpec((3, XC, BLK, LANES), lambda b, c, r: (0, c, b, 0)),
            ],
            out_specs=block,
            scratch_shapes=[pltpu.VMEM((66, 80, LANES), F32)] * 3
            + [
                pltpu.VMEM((2, 80, LANES), F32),
                pltpu.VMEM((384, 256), BF16),
                pltpu.VMEM((4, rows, LANES), BF16),
                pltpu.SemaphoreType.DMA((4,)),
            ],
        ),
        compiler_params=pltpu.CompilerParams(vmem_limit_bytes=LIMIT),
        cost_estimate=pl.CostEstimate(flops=60 << 20, bytes_accessed=22 << 20, transcendentals=0),
        name="warp",
    )(tab, own, far, fixed, field)


def put_planes(is_warped, g, count, start, total, diff, value, value_y, fixed, fixed_y):
    def step(i, carry):
        f, v = fixed[i].astype(F32), value[i].astype(F32)
        fy, vy = fixed_y[i].astype(F32), value_y[i].astype(F32)
        fy = jnp.where(g == 1, fy[8:16], fy[0:8])
        if vy.shape[0] == 16:
            vy = jnp.where(g == 1, vy[8:16], vy[0:8])
        if is_warped:
            s, m, sy, my = f + v, f - v, fy + vy, fy - vy
        else:
            s, m, sy, my = 2.0 * f - v, v, 2.0 * fy - vy, vy
        zero = jnp.zeros_like(sy)
        j = start + i
        total[j, 16:144, :] = s
        diff[j, 16:144, :] = m
        total[j, 8:16, :] = jnp.where(g == 1, sy, zero)
        total[j, 144:152, :] = jnp.where(g == 0, sy, zero)
        diff[j, 8:16, :] = jnp.where(g == 1, my, zero)
        diff[j, 144:152, :] = jnp.where(g == 0, my, zero)
        return carry

    lax.fori_loop(0, count, step, 0)


def update_planes(g, count, base, start, total, diff, summed, prior, prior_y, source):
    lane = lane_of((8, LANES))

    def step(i, carry):
        j = start + i
        for t in range(18):
            r = 8 + 8 * t
            here = total[j, r : r + 8, :]
            gx = total[j + 1, r : r + 8, :] - total[j - 1, r : r + 8, :]
            gy = total[j, r + 1 : r + 9, :] - total[j, r - 1 : r + 7, :]
            gz = jnp.where(lane < LANES - 1, pltpu.roll(here, LANES - 1, 1), 0.0) - jnp.where(
                lane > 0, pltpu.roll(here, 1, 1), 0.0
            )
            m = diff[j, r : r + 8, :]
            size = (gx * gx + gy * gy) + (gz * gz + (16.0 * m * m + 16.0 * STIFF))
            inv = pl.reciprocal(size, approx=True)
            inv = inv * (2.0 - size * inv)
            scale = (4.0 * m) * inv
            for c, grad in enumerate((gx, gy, gz)):
                value = scale * grad
                if prior is not None:
                    if 1 <= t <= 16:
                        value = value + prior[c, source + i, 8 * t - 8 : 8 * t, :]
                    else:
                        own = (g == 1) if t == 0 else (g == 0)
                        value = value + jnp.where(own, prior_y[c, source + i, 0:8, :], 0.0)
                summed[c, base + i, r - 8 : r, :] = value
        return carry

    lax.fori_loop(0, count, step, 0, unroll=4)


def smooth_planes(before, after, summed, along, wide, weights, out):
    w = [float(v) for v in taps()]

    def tap_sum(values):
        acc = w[RADIUS] * values[RADIUS]
        for k in range(RADIUS):
            acc = acc + w[k] * (values[k] + values[2 * RADIUS - k])
        return acc

    def rows(t, carry):
        r = pl.ds(pl.multiple_of(8 * t, 8), 8)
        for c in range(3):
            planes = [summed[c, before + j, r, :] for j in range(CH)]
            planes += [summed[c, after + j, r, :] for j in range(CH)]
            for o in range(CH):
                along[c, o, r, :] = tap_sum(planes[o : o + 2 * RADIUS + 1])
        return carry

    lax.fori_loop(0, 18, rows, 0, unroll=2)

    for o in range(CH):
        lhs = wide.at[o]
        for c in range(3):
            for t in range(8):
                r = 16 * t + 4
                acc = tap_sum([along[c, o, r + k : r + k + 16, :] for k in range(2 * RADIUS + 1)])
                high = acc.astype(BF16)
                lhs[c * 128 + 16 * t : c * 128 + 16 * t + 16, 0:LANES] = high
                lhs[c * 128 + 16 * t : c * 128 + 16 * t + 16, LANES:] = (acc - high.astype(F32)).astype(BF16)
        got = jnp.dot(lhs[...], weights[...], preferred_element_type=F32)
        for c in range(3):
            part = got[c * 128 : c * 128 + 128]
            out[c, o] = part[:, :LANES] + part[:, LANES:]


def scratch(planes):
    return [
        pltpu.VMEM((planes, 160, LANES), F32),
        pltpu.VMEM((planes, 160, LANES), F32),
        pltpu.VMEM((3, 16, 144, LANES), F32),
        pltpu.VMEM((3, CH, 144, LANES), F32),
        pltpu.VMEM((CH, 384, 256), BF16),
    ]


def inner_body(table, is_warped, ref, weights, value, value_y, fixed, fixed_y, *refs):
    prior, prior_y = (None, None) if is_warped else refs[:2]
    out, total, diff, summed, along, wide = refs[0 if is_warped else 2 :]
    k = pl.program_id(0)
    g = table.row(ref)
    cur = lax.rem(k, 2) * CH
    put_planes(is_warped, g, CH + 2, 0, total, diff, value, value_y, fixed, fixed_y)
    update_planes(g, CH, cur, 1, total, diff, summed, prior, prior_y, 0)

    @pl.when(k > 0)
    def _():
        smooth_planes(CH - cur, cur, summed, along, wide, weights, out)


def inner(table, tab, weights, value, value_y, fixed, fixed_y, prior=None, prior_y=None):
    tile_x = fixed.shape[0]
    is_warped = prior is None

    def window(array, planes, first):
        dims = array.shape
        if len(dims) == 3:
            return pl.BlockSpec(
                (pl.Element(planes), pl.Element(dims[1]), pl.Element(dims[2])), lambda k, r: (k * CH + first, 0, 0)
            )
        return pl.BlockSpec(
            (pl.Element(dims[0]), pl.Element(planes), pl.Element(dims[2]), pl.Element(dims[3])),
            lambda k, r: (0, k * CH + first, 0, 0),
        )

    specs = [pl.BlockSpec(weights.shape, lambda k, r: (0, 0))]
    args = [weights]
    for array in (value, value_y, fixed, fixed_y):
        specs.append(window(array, CH + 2, 3))
        args.append(array)
    if not is_warped:
        for array in (prior, prior_y):
            specs.append(window(array, CH, 4))
            args.append(array)
    return pl.pallas_call(
        functools.partial(inner_body, table, is_warped),
        out_shape=jax.ShapeDtypeStruct((3,) + fixed.shape, F32),
        grid_spec=pltpu.PrefetchScalarGridSpec(
            num_scalar_prefetch=1,
            grid=(tile_x // CH - 1,),
            in_specs=specs,
            out_specs=pl.BlockSpec((3, CH) + fixed.shape[1:], lambda k, r: (0, jnp.maximum(k, 1), 0, 0)),
            scratch_shapes=scratch(CH + 2),
        ),
        compiler_params=pltpu.CompilerParams(vmem_limit_bytes=LIMIT),
        cost_estimate=pl.CostEstimate(flops=200 << 20, bytes_accessed=30 << 20, transcendentals=0),
        name="inner%d" % (not is_warped),
    )(tab, *args)


def rim_body(table, is_warped, ref, weights, value, value_y, fixed, fixed_y, *refs):
    halo = refs[:4]
    refs = refs[4:]
    if is_warped:
        prior = prior_y = None
    else:
        prior, prior_y, prior_low, prior_high = refs[:4]
        refs = refs[4:]
    _, out, total, diff, summed, along, wide = refs
    k = pl.program_id(0)
    g = table.row(ref)
    put_planes(is_warped, g, 13, 5 * (1 - k), total, diff, value, value_y, fixed, fixed_y)

    def side(at, value_x, fixed_x):
        v_main, v_y = value_x.at[:5, :128, :], value_x.at[:5, 128:, :]
        f_main, f_y = fixed_x.at[5:, :128, :], fixed_x.at[5:, 128:, :]
        put_planes(is_warped, g, 5, at, total, diff, v_main, v_y, f_main, f_y)

    @pl.when(k == 0)
    def _():
        side(0, halo[0], halo[2])

    @pl.when(k == 1)
    def _():
        side(13, halo[1], halo[3])

    if is_warped:
        update_planes(g, 16, 0, 1, total, diff, summed, None, None, 0)
    else:
        update_planes(g, 12, 4 * (1 - k), 1 + 4 * (1 - k), total, diff, summed, prior, prior_y, 0)

        def outside(at, prior_x):
            update_planes(
                g, 4, at, 1 + at, total, diff, summed, prior_x.at[:, :, :128, :], prior_x.at[:, :, 128:, :], 0
            )

        @pl.when(k == 0)
        def _():
            outside(0, prior_low)

        @pl.when(k == 1)
        def _():
            outside(12, prior_high)

    smooth_planes(0, CH, summed, along, wide, weights, out)


def rim(table, tab, weights, field, value, value_y, fixed, fixed_y, halo, prior=None, prior_y=None, prior_x=()):
    tile_x = fixed.shape[0]
    is_warped = prior is None

    def window(array, planes):
        dims = array.shape
        if len(dims) == 3:
            return pl.BlockSpec(
                (pl.Element(planes), pl.Element(dims[1]), pl.Element(dims[2])),
                lambda k, r: (k * (tile_x - planes), 0, 0),
            )
        return pl.BlockSpec(
            (pl.Element(dims[0]), pl.Element(planes), pl.Element(dims[2]), pl.Element(dims[3])),
            lambda k, r: (0, k * (tile_x - planes), 0, 0),
        )

    def whole(array):
        return pl.BlockSpec(array.shape, lambda k, r: (0,) * array.ndim)

    specs, args = [whole(weights)], [weights]
    for array in (value, value_y, fixed, fixed_y):
        specs.append(window(array, 13))
        args.append(array)
    for array in halo:
        specs.append(whole(array))
        args.append(array)
    if not is_warped:
        for array in (prior, prior_y):
            specs.append(window(array, 12))
            args.append(array)
        for array in prior_x:
            specs.append(whole(array))
            args.append(array)
    specs.append(pl.BlockSpec(memory_space=pl.ANY))
    args.append(field)
    last = tile_x // CH - 1
    return pl.pallas_call(
        functools.partial(rim_body, table, is_warped),
        out_shape=jax.ShapeDtypeStruct(field.shape, F32),
        grid_spec=pltpu.PrefetchScalarGridSpec(
            num_scalar_prefetch=1,
            grid=(2,),
            in_specs=specs,
            out_specs=pl.BlockSpec((3, CH) + fixed.shape[1:], lambda k, r: (0, k * last, 0, 0)),
            scratch_shapes=scratch(18),
        ),
        input_output_aliases={len(args): 0},
        compiler_params=pltpu.CompilerParams(vmem_limit_bytes=LIMIT),
        cost_estimate=pl.CostEstimate(flops=60 << 20, bytes_accessed=10 << 20, transcendentals=0),
        name="rim%d" % (not is_warped),
    )(tab, *args)


def swap_y(values, g, rows):
    def edge(value):
        axis, length = value.ndim - 2, value.shape[-2]
        first = lax.slice_in_dim(value, 0, rows, axis=axis)
        last = lax.slice_in_dim(value, length - rows, length, axis=axis)
        return jnp.where(g == 0, last, first)

    edges = [edge(value) for value in values]
    return lax.ppermute(jnp.concatenate(edges) if len(edges) > 1 else edges[0], "gy", [(0, 1), (1, 0)])


def shift_x(pairs, width):
    size = lax.axis_size("gx")
    up = [(i, i + 1) for i in range(size - 1)]
    down = [(j, i) for i, j in up]

    def part(end):
        faces = []
        for pair in pairs:
            axis = pair[0].ndim - 3
            start = pair[0].shape[axis] - width if end else 0
            rows = [lax.slice_in_dim(v, start, start + width, axis=axis) for v in pair]
            faces.append(jnp.concatenate(rows, axis=axis + 1))
        return jnp.concatenate(faces) if len(faces) > 1 else faces[0]

    return lax.ppermute(part(True), "gx", up), lax.ppermute(part(False), "gx", down)


def column_body(table, ref, low, main, high, rows_y, out):
    g = table.row(ref)
    lane = lane_of((128, LANES))
    small = lane_of((16, LANES))

    def put(i, acc, plane, plane_y):
        shift = lax.rem(i + 256 - (BLK - 1), LANES)
        got = pltpu.roll(plane, shift, 1)
        got_y = pltpu.roll(plane_y, shift, 1)
        return (
            jnp.where(lane == i, got, acc[0]),
            jnp.where(lane == i + 1, got, acc[1]),
            jnp.where(small == i, got_y, acc[2]),
            jnp.where(small == i + 1, got_y, acc[3]),
        )

    acc = (jnp.zeros((128, LANES), F32),) * 2 + (jnp.zeros((16, LANES), F32),) * 2
    acc = put(0, acc, low[0].astype(F32), rows_y[0].astype(F32))
    acc = put(65, acc, high[0].astype(F32), rows_y[65].astype(F32))

    def step(x, acc):
        return put(x + 1, acc, main[x].astype(F32), rows_y[x + 1].astype(F32))

    acc = lax.fori_loop(0, 64, step, acc)
    for k in range(2):
        full, part = acc[k], acc[2 + k]
        if k:
            full, part = pltpu.roll(full, LANES - 1, 1), pltpu.roll(part, LANES - 1, 1)
        out[k, 16:144, :] = full.astype(BF16)
        out[k, 0:16, :] = jnp.where(g == 1, part, 0.0).astype(BF16)
        out[k, 144:160, :] = jnp.where(g == 0, part, 0.0).astype(BF16)


def columns(table, tab, low, main, high, rows_y):
    args = (low, main, high, rows_y)
    return pl.pallas_call(
        functools.partial(column_body, table),
        out_shape=jax.ShapeDtypeStruct((2, 160, LANES), BF16),
        grid_spec=pltpu.PrefetchScalarGridSpec(
            num_scalar_prefetch=1,
            grid=(1,),
            in_specs=[pl.BlockSpec(v.shape, lambda d, r: (0, 0, 0)) for v in args],
            out_specs=pl.BlockSpec((2, 160, LANES), lambda d, r: (0, 0, 0)),
        ),
        compiler_params=pltpu.CompilerParams(vmem_limit_bytes=LIMIT),
        cost_estimate=SMALL,
        name="columns",
    )(tab, *args)


def shell_rows(low, main, high, rows_y, column, g):
    def at(y):
        return jnp.concatenate([low[:, y], main[:, y], high[:, y]])

    below = [jnp.where(g == 1, rows_y[:, -1], 0), at(BLK - 1)]
    above = [at(BLK), jnp.where(g == 0, rows_y[:, 0], 0)]
    faces = []
    for b in range(2):
        y = slice(b * BLK, b * BLK + BLK)
        for c in range(2):
            z = slice(c * BLK, c * BLK + BLK)
            side_x = jnp.concatenate([low[0, y, z], high[0, y, z]], axis=1)
            side_y = jnp.concatenate([below[b][:, z], above[b][:, z]], axis=1)
            side_z = column[1 - c, b * BLK + 8 : b * BLK + 88]
            faces.append(jnp.concatenate([side_x, jnp.pad(side_y, ((0, 14), (0, 0))), side_z], axis=0))
    return jnp.stack(faces)


def local(fixed, moving, source_x, source_z):
    g = lax.axis_index("gy")
    table = Table(source_x.shape)
    tab = jnp.concatenate(
        [
            source_x.reshape(-1),
            source_z.reshape(-1),
            jnp.stack([lax.axis_index("gx"), g]).astype(jnp.int32),
        ]
    )
    weights = band()
    n = lax.axis_size("gx")
    half = n // 2
    opposite = [(i, (i + half) % n) for i in range(n)]
    halves = [list(range(half)), list(range(half, n))]

    def send(slots):
        return lax.all_to_all(slots, "gx", split_axis=0, concat_axis=0, axis_index_groups=halves, tiled=True)

    tile_x = fixed.shape[0]
    hold = lax.optimization_barrier
    up = [(i, i + 1) for i in range(n - 1)]
    low = lax.ppermute(moving[-1:], "gx", up)
    high = lax.ppermute(moving[:1], "gx", [(j, i) for i, j in up])
    rows_y = swap_y([fixed, moving], g, 16)
    own0 = pack(table, tab, 0, False, [moving])
    first, low, high, rows_y, own0 = hold((moving, low, high, rows_y, own0))

    mirror_a = lax.ppermute(first[:PART], "gx", opposite)
    own0 = send(own0)
    rows_x = swap_y([low, high], g, 16)
    fixed_y = rows_y[:tile_x]
    moving_y = jnp.concatenate([rows_x[:1], rows_y[tile_x:], rows_x[1:]])
    column = columns(table, tab, low, moving, high, moving_y)
    shells = shell_rows(low, moving, high, moving_y, column, g)
    own1 = pack(table, tab, 1, False, [moving], shells)
    mirror_a, own0, own1, shells, rest = hold((mirror_a, own0, own1, shells, first[PART:]))

    mirror_b = lax.ppermute(rest, "gx", opposite)
    shells_far = lax.ppermute(shells, "gx", opposite)
    own1 = send(own1)
    mirror_b, shells_far, own1 = hold((mirror_b, shells_far, own1))

    far0 = send(pack(table, tab, 0, True, [mirror_a, mirror_b]))
    far1 = pack(table, tab, 1, True, [mirror_a, mirror_b], shells_far)
    _, far1 = hold((far0, far1))
    far1 = send(far1)

    warped = pick(table, tab, 0, own0, far0, fixed.shape)
    warped_y = swap_y([warped], g, 16)
    faces_x = shift_x([(warped, warped_y), (fixed, fixed_y)], 5)
    field = inner(table, tab, weights, warped, warped_y, fixed, fixed_y)
    field = rim(table, tab, weights, field, warped, warped_y, fixed, fixed_y, (*faces_x, *faces_x))
    field_y = swap_y([field], g, 8)
    field_x = shift_x([(field, field_y)], 4)

    mismatch = warp(table, tab, 1, own1, far1, fixed, field)
    mismatch_y = swap_y([mismatch], g, 8)
    mismatch_x = shift_x([(mismatch, mismatch_y)], 5)
    last = inner(table, tab, weights, mismatch, mismatch_y, fixed, fixed_y, field, field_y)
    last = rim(
        table, tab, weights, last, mismatch, mismatch_y, fixed, fixed_y, (*mismatch_x, *faces_x), field, field_y, field_x
    )
    return (last, mismatch)


def solution(mesh):
    return jax.shard_map(
        local,
        mesh=mesh,
        in_specs=(
            P(("groups", "gx"), "gy", None),
            P(("groups", "gx"), "gy", None),
            P("groups", None, None, None),
            P("groups", None, None, None),
        ),
        out_specs=(P(None, ("groups", "gx"), "gy", None), P(("groups", "gx"), "gy", None)),
        check_vma=False,
    )
```

```python
import functools

import jax
import jax.numpy as jnp
import numpy as np
from jax import lax
from jax.experimental import pallas as pl
from jax.experimental.pallas import tpu as pltpu
from jax.sharding import PartitionSpec as P

BLK = 64
RADIUS = 4
STIFF = 0.05
LANES = 128
CH = 8
LARGE = pl.CostEstimate(flops=1 << 27, bytes_accessed=1 << 27, transcendentals=0)
SMALL = pl.CostEstimate(flops=1 << 16, bytes_accessed=1 << 16, transcendentals=0)
LIMIT = 56 * 1024 * 1024
F32 = jnp.float32
BF16 = jnp.bfloat16


def taps():
    k = np.arange(-RADIUS, RADIUS + 1).astype(np.float32)
    w = np.exp(-k * k / np.float32(4.5)).astype(np.float32)
    return (w / np.sum(w)).astype(np.float32)


def band():
    w = taps()
    full = np.zeros((LANES, LANES), np.float32)
    for i in range(LANES):
        for k in range(-RADIUS, RADIUS + 1):
            if 0 <= i + k < LANES:
                full[i + k, i] = w[k + RADIUS]
    high = jnp.asarray(full).astype(BF16)
    low = (jnp.asarray(full) - high.astype(F32)).astype(BF16)
    row = jnp.concatenate([high, low], 1)
    return jnp.concatenate([row, row], 0)


def lane_of(shape):
    return lax.broadcasted_iota(jnp.int32, shape, len(shape) - 1)


class Table:
    def __init__(self, shape):
        self.shape = shape
        self.size = int(np.prod(shape))

    def at(self, t, d, b, c):
        _, n, yb, zb = self.shape
        return ((t * n + d) * yb + b) * zb + c

    def x(self, ref, t, d, b, c):
        return ref[self.at(t, d, b, c)]

    def z(self, ref, t, d, b, c):
        return ref[self.size + self.at(t, d, b, c)]

    def column(self, ref):
        return ref[2 * self.size]

    def row(self, ref):
        return ref[2 * self.size + 1]


def wanted_block(table, ref, t, d, column):
    g = table.row(ref)
    blk_y, blk_z, out_z = jnp.int32(0), jnp.int32(0), jnp.int32(0)
    for b in range(2):
        for c in range(2):
            hit = table.x(ref, t, d, g * 2 + b, c) == column
            blk_y = jnp.where(hit, b, blk_y)
            blk_z = jnp.where(hit, table.z(ref, t, d, g * 2 + b, c), blk_z)
            out_z = jnp.where(hit, c, out_z)
    return blk_y, blk_z, out_z


MAIN = 32 * BLK
GROUP = 8
PART = 32


def pack_body(table, t, far, count, shell, ref, *refs):
    n = table.shape[1]
    half = n // 2
    a = table.column(ref)
    here = (a >= half).astype(jnp.int32)
    column = a if not far else jnp.where(a >= half, a - half, a + half)
    blk_y, blk_z, out_z = wanted_block(table, ref, t, here * half + pl.program_id(0), column)
    parts, out = refs[:count], refs[-1]
    y0 = pl.multiple_of(blk_y * BLK, BLK)
    keep = (lane_of((GROUP, BLK, LANES)) < 64) == (blk_z == 0)
    turn = jnp.where(blk_z == out_z, 0, PART // 2)
    for k, mov in enumerate(parts):
        for x in range(0, PART // 2, GROUP):
            same = mov[pl.ds(x + turn, GROUP), pl.ds(y0, BLK), :]
            other = mov[pl.ds(x + PART // 2 - turn, GROUP), pl.ds(y0, BLK), :]
            other = pltpu.roll(other.reshape(GROUP * BLK, LANES), 64, 1).reshape(GROUP, BLK, LANES)
            got = jnp.where(keep, same.astype(F32), other.astype(F32)).astype(BF16)
            row = (k * PART // 2 + x) * BLK
            out[0, row : row + GROUP * BLK, :] = got.reshape(GROUP * BLK, LANES)
    if shell:
        out[0, MAIN:, :] = refs[count][blk_y * 2 + blk_z]


def pack(table, tab, t, far, parts, shells=None):
    half = table.shape[1] // 2
    args, specs = [], []
    for part in parts:
        for i in range(part.shape[0] // PART):
            args.append(part)
            specs.append(pl.BlockSpec((PART,) + part.shape[1:], lambda d, r, i=i: (i, 0, 0)))
    count = len(args)
    rows = count * PART // 2 * BLK
    if shells is not None:
        rows = rows + shells.shape[1]
        args.append(shells)
        specs.append(pl.BlockSpec(shells.shape, lambda d, r: (0, 0, 0)))
    return pl.pallas_call(
        functools.partial(pack_body, table, t, far, count, shells is not None),
        out_shape=jax.ShapeDtypeStruct((half, rows, LANES), BF16),
        grid_spec=pltpu.PrefetchScalarGridSpec(
            num_scalar_prefetch=1,
            grid=(half,),
            in_specs=specs,
            out_specs=pl.BlockSpec((1, rows, LANES), lambda d, r: (d, 0, 0)),
        ),
        compiler_params=pltpu.CompilerParams(vmem_limit_bytes=LIMIT),
        cost_estimate=LARGE if t == 1 and far else SMALL,
        name="pack%d%s" % (t, "far" if far else "own"),
    )(tab, *args)


def fetch(table, t, ref, own, far, slots, sems):
    n = table.shape[1]
    half = n // 2
    a, g = table.column(ref), table.row(ref)
    for b in range(2):
        for c in range(2):
            source = table.x(ref, t, a, g * 2 + b, c)
            near = (source >= half) == (a >= half)
            index = jnp.where(source >= half, source - half, source)
            k = 2 * b + c

            @pl.when(near)
            def _():
                pltpu.make_async_copy(own(index), slots.at[k], sems.at[k]).start()

            @pl.when(jnp.logical_not(near))
            def _():
                pltpu.make_async_copy(far(index), slots.at[k], sems.at[k]).start()


def await_slot(own, slots, sems, k):
    pltpu.make_async_copy(own(0), slots.at[k], sems.at[k]).wait()


def main_rows(p, q, put_first, put_second):
    low = lane_of((GROUP * BLK, LANES)) < 64

    def step(i, carry):
        row = i * GROUP
        rows = pl.ds(pl.multiple_of(row * BLK, GROUP * BLK), GROUP * BLK)
        u, v = p[rows, :].astype(F32), q[rows, :].astype(F32)
        x = row + lax.div(row, PART // 2) * (PART // 2)
        put_first(x, jnp.where(low, u, v).reshape(GROUP, BLK, LANES))
        second = pltpu.roll(jnp.where(low, v, u).astype(BF16), 64, 1)
        put_second(x + PART // 2, second.reshape(GROUP, BLK, LANES))
        return carry

    lax.fori_loop(0, 32 // GROUP, step, 0)


def pick_body(table, t, ref, own_ref, far_ref, out, slots, sems):
    b = pl.program_id(0)
    own, far = lambda i: own_ref.at[i], lambda i: far_ref.at[i]

    @pl.when(b == 0)
    def _():
        fetch(table, t, ref, own, far, slots, sems)

    await_slot(own, slots, sems, 2 * b)
    await_slot(own, slots, sems, 2 * b + 1)

    def put(x, value):
        out[pl.ds(x, GROUP)] = value.astype(BF16)

    main_rows(slots.at[2 * b], slots.at[2 * b + 1], put, put)


def pick(table, tab, t, own, far, shape):
    rows = own.shape[1]
    return pl.pallas_call(
        functools.partial(pick_body, table, t),
        out_shape=jax.ShapeDtypeStruct(shape, BF16),
        grid_spec=pltpu.PrefetchScalarGridSpec(
            num_scalar_prefetch=1,
            grid=(2,),
            in_specs=[pl.BlockSpec(memory_space=pl.ANY)] * 2,
            out_specs=pl.BlockSpec((64, BLK, LANES), lambda b, r: (0, b, 0)),
            scratch_shapes=[pltpu.VMEM((4, rows, LANES), BF16), pltpu.SemaphoreType.DMA((4,))],
        ),
        compiler_params=pltpu.CompilerParams(vmem_limit_bytes=LIMIT),
        cost_estimate=pl.CostEstimate(flops=2 * 64 * 128 * 128, bytes_accessed=4 << 20, transcendentals=0),
        name="pick",
    )(tab, own, far)


XC = 16
SPAN = 8


def warp_body(table, t, ref, own_ref, far_ref, fixed, field, out, near, up, down, edge, turn, slots, sems):
    b, chunk = pl.program_id(0), pl.program_id(1)
    own, far = lambda i: own_ref.at[i], lambda i: far_ref.at[i]

    @pl.when((b == 0) & (chunk == 0))
    def _():
        fetch(table, t, ref, own, far, slots, sems)

    def widen(first, count):
        face_p = slots[2 * b, MAIN + 144 : MAIN + 224, :].astype(F32)
        face_q = slots[2 * b + 1, MAIN + 144 : MAIN + 224, :].astype(F32)
        lane = lane_of((80, LANES))
        parts = []
        for k in range(count):
            i = first + k
            near[i, 7:8, :] = edge[0, pl.ds(i, 1), :]
            near[i, 72:73, :] = edge[1, pl.ds(i, 1), :]
            here = lane == i
            sides = [jnp.where(here, face, 0.0).astype(BF16) for face in (face_p, face_q)]
            parts.append(jnp.concatenate([near[i].astype(BF16)] + sides, axis=1))
        got = jnp.dot(jnp.concatenate(parts, axis=0), turn[...], preferred_element_type=F32)
        got = got.reshape(count, 80, 256)
        up[pl.ds(first, count)] = got[:, :, :LANES]
        down[pl.ds(first, count)] = got[:, :, LANES:]

    @pl.when(chunk == 0)
    def _():
        await_slot(own, slots, sems, 2 * b)
        await_slot(own, slots, sems, 2 * b + 1)
        p, q = slots.at[2 * b], slots.at[2 * b + 1]

        def put(x, value):
            near[pl.ds(x + 1, GROUP), 8:72, :] = value.astype(F32)

        main_rows(p, q, put, put)

        def both(start, size):
            u = p[start : start + size, :].astype(F32)
            v = q[start : start + size, :].astype(F32)
            mask = lane_of((size, LANES)) < 64
            return jnp.where(mask, u, pltpu.roll(v, 64, 1)), jnp.where(mask, pltpu.roll(u, 64, 1), v)

        first, second = both(MAIN, BLK)
        near[0, 8:72, :] = first
        near[65, 8:72, :] = second
        first, second = both(MAIN + 64, 80)
        edge[0] = first
        edge[1] = second

        a, g = table.column(ref), table.row(ref)
        z_p = table.z(ref, t, a, g * 2 + b, 0)
        z_q = table.z(ref, t, a, g * 2 + b, 1)
        row = lax.broadcasted_iota(jnp.int32, (128, 256), 0)
        col = lax.broadcasted_iota(jnp.int32, (128, 256), 1)
        inside = ((row == col + 1) & (col != 63)) | ((row == col - 129) & (col != 192))
        turn[0:128, :] = jnp.where(inside, 1.0, 0.0).astype(BF16)
        turn[128:256, :] = jnp.where(col == jnp.where(z_p == 0, 63, 128), 1.0, 0.0).astype(BF16)
        turn[256:384, :] = jnp.where(col == jnp.where(z_q == 0, 127, 192), 1.0, 0.0).astype(BF16)
        widen(0, 2)

    for start in range(0, XC, SPAN):
        widen(chunk * XC + 2 + start, SPAN)

    def planes(j, carry):
        for tile in range(8):
            r = 8 * tile
            seen = {}

            def load(name, array, xi, ky):
                if (name, xi, ky) not in seen:
                    y0 = 7 + r + ky
                    seen[name, xi, ky] = array[chunk * XC + 4 * j + xi, y0 : y0 + 8, :]
                return seen[name, xi, ky]

            for xo in range(4):
                x = 4 * j + xo
                fx, fy, fz = field[0, x, r : r + 8, :], field[1, x, r : r + 8, :], field[2, x, r : r + 8, :]
                px, py, pz = fx > 0, fy > 0, fz > 0
                wx, wy, wz = jnp.abs(fx), jnp.abs(fy), jnp.abs(fz)
                per_x = []
                for kx in range(3):
                    per_y = []
                    for ky in range(3):
                        here = load("near", near, xo + kx, ky)
                        beside = jnp.where(pz, load("up", up, xo + kx, ky), load("down", down, xo + kx, ky))
                        per_y.append((here, beside))
                    aside = [jnp.where(py, per_y[2][i], per_y[0][i]) for i in range(2)]
                    per_x.append((per_y[1], aside))
                lines = []
                for s in range(2):
                    c00, c01, c10, c11 = [
                        per_x[1][v][i] if s == 0 else jnp.where(px, per_x[2][v][i], per_x[0][v][i])
                        for v in range(2)
                        for i in range(2)
                    ]
                    l0 = c00 + wz * (c01 - c00)
                    l1 = c10 + wz * (c11 - c10)
                    lines.append(l0 + wy * (l1 - l0))
                warped = lines[0] + wx * (lines[1] - lines[0])
                out[x, r : r + 8, :] = fixed[x, r : r + 8, :].astype(F32) - warped
        return carry

    lax.fori_loop(0, XC // 4, planes, 0)


def warp(table, tab, t, own, far, fixed, field):
    rows = own.shape[1]
    tile_x = fixed.shape[0]
    block = pl.BlockSpec((XC, BLK, LANES), lambda b, c, r: (c, b, 0))
    return pl.pallas_call(
        functools.partial(warp_body, table, t),
        out_shape=jax.ShapeDtypeStruct(fixed.shape, F32),
        grid_spec=pltpu.PrefetchScalarGridSpec(
            num_scalar_prefetch=1,
            grid=(2, tile_x // XC),
            in_specs=[
                pl.BlockSpec(memory_space=pl.ANY),
                pl.BlockSpec(memory_space=pl.ANY),
                block,
                pl.BlockSpec((3, XC, BLK, LANES), lambda b, c, r: (0, c, b, 0)),
            ],
            out_specs=block,
            scratch_shapes=[pltpu.VMEM((66, 80, LANES), F32)] * 3
            + [
                pltpu.VMEM((2, 80, LANES), F32),
                pltpu.VMEM((384, 256), BF16),
                pltpu.VMEM((4, rows, LANES), BF16),
                pltpu.SemaphoreType.DMA((4,)),
            ],
        ),
        compiler_params=pltpu.CompilerParams(vmem_limit_bytes=LIMIT),
        cost_estimate=pl.CostEstimate(flops=60 << 20, bytes_accessed=22 << 20, transcendentals=0),
        name="warp",
    )(tab, own, far, fixed, field)


def put_planes(is_warped, g, count, start, total, diff, value, value_y, fixed, fixed_y):
    def step(i, carry):
        f, v = fixed[i].astype(F32), value[i].astype(F32)
        fy, vy = fixed_y[i].astype(F32), value_y[i].astype(F32)
        fy = jnp.where(g == 1, fy[8:16], fy[0:8])
        if vy.shape[0] == 16:
            vy = jnp.where(g == 1, vy[8:16], vy[0:8])
        if is_warped:
            s, m, sy, my = f + v, f - v, fy + vy, fy - vy
        else:
            s, m, sy, my = 2.0 * f - v, v, 2.0 * fy - vy, vy
        zero = jnp.zeros_like(sy)
        j = start + i
        total[j, 16:144, :] = s
        diff[j, 16:144, :] = m
        total[j, 8:16, :] = jnp.where(g == 1, sy, zero)
        total[j, 144:152, :] = jnp.where(g == 0, sy, zero)
        diff[j, 8:16, :] = jnp.where(g == 1, my, zero)
        diff[j, 144:152, :] = jnp.where(g == 0, my, zero)
        return carry

    lax.fori_loop(0, count, step, 0, unroll=count)


def update_planes(g, count, base, start, total, diff, summed, prior, prior_y, source):
    lane = lane_of((8, LANES))

    def step(i, carry):
        j = start + i
        for t in range(18):
            r = 8 + 8 * t
            here = total[j, r : r + 8, :]
            gx = total[j + 1, r : r + 8, :] - total[j - 1, r : r + 8, :]
            gy = total[j, r + 1 : r + 9, :] - total[j, r - 1 : r + 7, :]
            gz = jnp.where(lane < LANES - 1, pltpu.roll(here, LANES - 1, 1), 0.0) - jnp.where(
                lane > 0, pltpu.roll(here, 1, 1), 0.0
            )
            m = diff[j, r : r + 8, :]
            size = (gx * gx + gy * gy) + (gz * gz + (16.0 * m * m + 16.0 * STIFF))
            inv = pl.reciprocal(size, approx=True)
            inv = inv * (2.0 - size * inv)
            scale = (4.0 * m) * inv
            for c, grad in enumerate((gx, gy, gz)):
                value = scale * grad
                if prior is not None:
                    if 1 <= t <= 16:
                        value = value + prior[c, source + i, 8 * t - 8 : 8 * t, :]
                    else:
                        own = (g == 1) if t == 0 else (g == 0)
                        value = value + jnp.where(own, prior_y[c, source + i, 0:8, :], 0.0)
                summed[c, base + i, r - 8 : r, :] = value
        return carry

    lax.fori_loop(0, count, step, 0, unroll=4)


def smooth_planes(before, after, summed, along, wide, weights, out):
    w = [float(v) for v in taps()]

    def tap_sum(values):
        acc = w[RADIUS] * values[RADIUS]
        for k in range(RADIUS):
            acc = acc + w[k] * (values[k] + values[2 * RADIUS - k])
        return acc

    def rows(t, carry):
        r = pl.ds(pl.multiple_of(8 * t, 8), 8)
        for c in range(3):
            planes = [summed[c, before + j, r, :] for j in range(CH)]
            planes += [summed[c, after + j, r, :] for j in range(CH)]
            for o in range(CH):
                along[c, o, r, :] = tap_sum(planes[o : o + 2 * RADIUS + 1])
        return carry

    lax.fori_loop(0, 18, rows, 0, unroll=2)

    for o in range(CH):
        lhs = wide.at[o]
        for c in range(3):
            for t in range(8):
                r = 16 * t + 4
                acc = tap_sum([along[c, o, r + k : r + k + 16, :] for k in range(2 * RADIUS + 1)])
                high = acc.astype(BF16)
                lhs[c * 128 + 16 * t : c * 128 + 16 * t + 16, 0:LANES] = high
                lhs[c * 128 + 16 * t : c * 128 + 16 * t + 16, LANES:] = (acc - high.astype(F32)).astype(BF16)
        got = jnp.dot(lhs[...], weights[...], preferred_element_type=F32)
        for c in range(3):
            part = got[c * 128 : c * 128 + 128]
            out[c, o] = part[:, :LANES] + part[:, LANES:]


def scratch(planes):
    return [
        pltpu.VMEM((planes, 160, LANES), F32),
        pltpu.VMEM((planes, 160, LANES), F32),
        pltpu.VMEM((3, 16, 144, LANES), F32),
        pltpu.VMEM((3, CH, 144, LANES), F32),
        pltpu.VMEM((CH, 384, 256), BF16),
    ]


def inner_body(table, is_warped, ref, weights, value, value_y, fixed, fixed_y, *refs):
    prior, prior_y = (None, None) if is_warped else refs[:2]
    out, total, diff, summed, along, wide = refs[0 if is_warped else 2 :]
    k = pl.program_id(0)
    g = table.row(ref)
    cur = lax.rem(k, 2) * CH
    put_planes(is_warped, g, CH + 2, 0, total, diff, value, value_y, fixed, fixed_y)
    update_planes(g, CH, cur, 1, total, diff, summed, prior, prior_y, 0)

    @pl.when(k > 0)
    def _():
        smooth_planes(CH - cur, cur, summed, along, wide, weights, out)


def inner(table, tab, weights, value, value_y, fixed, fixed_y, prior=None, prior_y=None):
    tile_x = fixed.shape[0]
    is_warped = prior is None

    def window(array, planes, first):
        dims = array.shape
        if len(dims) == 3:
            return pl.BlockSpec(
                (pl.Element(planes), pl.Element(dims[1]), pl.Element(dims[2])), lambda k, r: (k * CH + first, 0, 0)
            )
        return pl.BlockSpec(
            (pl.Element(dims[0]), pl.Element(planes), pl.Element(dims[2]), pl.Element(dims[3])),
            lambda k, r: (0, k * CH + first, 0, 0),
        )

    specs = [pl.BlockSpec(weights.shape, lambda k, r: (0, 0))]
    args = [weights]
    for array in (value, value_y, fixed, fixed_y):
        specs.append(window(array, CH + 2, 3))
        args.append(array)
    if not is_warped:
        for array in (prior, prior_y):
            specs.append(window(array, CH, 4))
            args.append(array)
    return pl.pallas_call(
        functools.partial(inner_body, table, is_warped),
        out_shape=jax.ShapeDtypeStruct((3,) + fixed.shape, F32),
        grid_spec=pltpu.PrefetchScalarGridSpec(
            num_scalar_prefetch=1,
            grid=(tile_x // CH - 1,),
            in_specs=specs,
            out_specs=pl.BlockSpec((3, CH) + fixed.shape[1:], lambda k, r: (0, jnp.maximum(k, 1), 0, 0)),
            scratch_shapes=scratch(CH + 2),
        ),
        compiler_params=pltpu.CompilerParams(vmem_limit_bytes=LIMIT),
        cost_estimate=pl.CostEstimate(flops=200 << 20, bytes_accessed=30 << 20, transcendentals=0),
        name="inner%d" % (not is_warped),
    )(tab, *args)


def rim_body(table, is_warped, ref, weights, value, value_y, fixed, fixed_y, *refs):
    halo = refs[:4]
    refs = refs[4:]
    if is_warped:
        prior = prior_y = None
    else:
        prior, prior_y, prior_low, prior_high = refs[:4]
        refs = refs[4:]
    _, out, total, diff, summed, along, wide = refs
    k = pl.program_id(0)
    g = table.row(ref)
    put_planes(is_warped, g, 13, 5 * (1 - k), total, diff, value, value_y, fixed, fixed_y)

    def side(at, value_x, fixed_x):
        v_main, v_y = value_x.at[:5, :128, :], value_x.at[:5, 128:, :]
        f_main, f_y = fixed_x.at[5:, :128, :], fixed_x.at[5:, 128:, :]
        put_planes(is_warped, g, 5, at, total, diff, v_main, v_y, f_main, f_y)

    @pl.when(k == 0)
    def _():
        side(0, halo[0], halo[2])

    @pl.when(k == 1)
    def _():
        side(13, halo[1], halo[3])

    if is_warped:
        update_planes(g, 16, 0, 1, total, diff, summed, None, None, 0)
    else:
        update_planes(g, 12, 4 * (1 - k), 1 + 4 * (1 - k), total, diff, summed, prior, prior_y, 0)

        def outside(at, prior_x):
            update_planes(
                g, 4, at, 1 + at, total, diff, summed, prior_x.at[:, :, :128, :], prior_x.at[:, :, 128:, :], 0
            )

        @pl.when(k == 0)
        def _():
            outside(0, prior_low)

        @pl.when(k == 1)
        def _():
            outside(12, prior_high)

    smooth_planes(0, CH, summed, along, wide, weights, out)


def rim(table, tab, weights, field, value, value_y, fixed, fixed_y, halo, prior=None, prior_y=None, prior_x=()):
    tile_x = fixed.shape[0]
    is_warped = prior is None

    def window(array, planes):
        dims = array.shape
        if len(dims) == 3:
            return pl.BlockSpec(
                (pl.Element(planes), pl.Element(dims[1]), pl.Element(dims[2])),
                lambda k, r: (k * (tile_x - planes), 0, 0),
            )
        return pl.BlockSpec(
            (pl.Element(dims[0]), pl.Element(planes), pl.Element(dims[2]), pl.Element(dims[3])),
            lambda k, r: (0, k * (tile_x - planes), 0, 0),
        )

    def whole(array):
        return pl.BlockSpec(array.shape, lambda k, r: (0,) * array.ndim)

    specs, args = [whole(weights)], [weights]
    for array in (value, value_y, fixed, fixed_y):
        specs.append(window(array, 13))
        args.append(array)
    for array in halo:
        specs.append(whole(array))
        args.append(array)
    if not is_warped:
        for array in (prior, prior_y):
            specs.append(window(array, 12))
            args.append(array)
        for array in prior_x:
            specs.append(whole(array))
            args.append(array)
    specs.append(pl.BlockSpec(memory_space=pl.ANY))
    args.append(field)
    last = tile_x // CH - 1
    return pl.pallas_call(
        functools.partial(rim_body, table, is_warped),
        out_shape=jax.ShapeDtypeStruct(field.shape, F32),
        grid_spec=pltpu.PrefetchScalarGridSpec(
            num_scalar_prefetch=1,
            grid=(2,),
            in_specs=specs,
            out_specs=pl.BlockSpec((3, CH) + fixed.shape[1:], lambda k, r: (0, k * last, 0, 0)),
            scratch_shapes=scratch(18),
        ),
        input_output_aliases={len(args): 0},
        compiler_params=pltpu.CompilerParams(vmem_limit_bytes=LIMIT),
        cost_estimate=pl.CostEstimate(flops=60 << 20, bytes_accessed=10 << 20, transcendentals=0),
        name="rim%d" % (not is_warped),
    )(tab, *args)


def swap_y(values, g, rows):
    def edge(value):
        axis, length = value.ndim - 2, value.shape[-2]
        first = lax.slice_in_dim(value, 0, rows, axis=axis)
        last = lax.slice_in_dim(value, length - rows, length, axis=axis)
        return jnp.where(g == 0, last, first)

    edges = [edge(value) for value in values]
    return lax.ppermute(jnp.concatenate(edges) if len(edges) > 1 else edges[0], "gy", [(0, 1), (1, 0)])


def shift_x(pairs, width):
    size = lax.axis_size("gx")
    up = [(i, i + 1) for i in range(size - 1)]
    down = [(j, i) for i, j in up]

    def part(end):
        faces = []
        for pair in pairs:
            axis = pair[0].ndim - 3
            start = pair[0].shape[axis] - width if end else 0
            rows = [lax.slice_in_dim(v, start, start + width, axis=axis) for v in pair]
            faces.append(jnp.concatenate(rows, axis=axis + 1))
        return jnp.concatenate(faces) if len(faces) > 1 else faces[0]

    return lax.ppermute(part(True), "gx", up), lax.ppermute(part(False), "gx", down)


def column_body(table, ref, low, main, high, rows_y, out):
    g = table.row(ref)
    lane = lane_of((128, LANES))
    small = lane_of((16, LANES))

    def put(i, acc, plane, plane_y):
        shift = lax.rem(i + 256 - (BLK - 1), LANES)
        got = pltpu.roll(plane, shift, 1)
        got_y = pltpu.roll(plane_y, shift, 1)
        return (
            jnp.where(lane == i, got, acc[0]),
            jnp.where(lane == i + 1, got, acc[1]),
            jnp.where(small == i, got_y, acc[2]),
            jnp.where(small == i + 1, got_y, acc[3]),
        )

    acc = (jnp.zeros((128, LANES), F32),) * 2 + (jnp.zeros((16, LANES), F32),) * 2
    acc = put(0, acc, low[0].astype(F32), rows_y[0].astype(F32))
    acc = put(65, acc, high[0].astype(F32), rows_y[65].astype(F32))

    def step(x, acc):
        return put(x + 1, acc, main[x].astype(F32), rows_y[x + 1].astype(F32))

    acc = lax.fori_loop(0, 64, step, acc)
    for k in range(2):
        full, part = acc[k], acc[2 + k]
        if k:
            full, part = pltpu.roll(full, LANES - 1, 1), pltpu.roll(part, LANES - 1, 1)
        out[k, 16:144, :] = full.astype(BF16)
        out[k, 0:16, :] = jnp.where(g == 1, part, 0.0).astype(BF16)
        out[k, 144:160, :] = jnp.where(g == 0, part, 0.0).astype(BF16)


def columns(table, tab, low, main, high, rows_y):
    args = (low, main, high, rows_y)
    return pl.pallas_call(
        functools.partial(column_body, table),
        out_shape=jax.ShapeDtypeStruct((2, 160, LANES), BF16),
        grid_spec=pltpu.PrefetchScalarGridSpec(
            num_scalar_prefetch=1,
            grid=(1,),
            in_specs=[pl.BlockSpec(v.shape, lambda d, r: (0, 0, 0)) for v in args],
            out_specs=pl.BlockSpec((2, 160, LANES), lambda d, r: (0, 0, 0)),
        ),
        compiler_params=pltpu.CompilerParams(vmem_limit_bytes=LIMIT),
        cost_estimate=SMALL,
        name="columns",
    )(tab, *args)


def shell_rows(low, main, high, rows_y, column, g):
    def at(y):
        return jnp.concatenate([low[:, y], main[:, y], high[:, y]])

    below = [jnp.where(g == 1, rows_y[:, -1], 0), at(BLK - 1)]
    above = [at(BLK), jnp.where(g == 0, rows_y[:, 0], 0)]
    faces = []
    for b in range(2):
        y = slice(b * BLK, b * BLK + BLK)
        for c in range(2):
            z = slice(c * BLK, c * BLK + BLK)
            side_x = jnp.concatenate([low[0, y, z], high[0, y, z]], axis=1)
            side_y = jnp.concatenate([below[b][:, z], above[b][:, z]], axis=1)
            side_z = column[1 - c, b * BLK + 8 : b * BLK + 88]
            faces.append(jnp.concatenate([side_x, jnp.pad(side_y, ((0, 14), (0, 0))), side_z], axis=0))
    return jnp.stack(faces)


def local(fixed, moving, source_x, source_z):
    g = lax.axis_index("gy")
    table = Table(source_x.shape)
    tab = jnp.concatenate(
        [
            source_x.reshape(-1),
            source_z.reshape(-1),
            jnp.stack([lax.axis_index("gx"), g]).astype(jnp.int32),
        ]
    )
    weights = band()
    n = lax.axis_size("gx")
    half = n // 2
    opposite = [(i, (i + half) % n) for i in range(n)]
    halves = [list(range(half)), list(range(half, n))]

    def send(slots):
        return lax.all_to_all(slots, "gx", split_axis=0, concat_axis=0, axis_index_groups=halves, tiled=True)

    tile_x = fixed.shape[0]
    hold = lax.optimization_barrier
    up = [(i, i + 1) for i in range(n - 1)]
    low = lax.ppermute(moving[-1:], "gx", up)
    high = lax.ppermute(moving[:1], "gx", [(j, i) for i, j in up])
    rows_y = swap_y([fixed, moving], g, 16)
    own0 = pack(table, tab, 0, False, [moving])
    first, low, high, rows_y, own0 = hold((moving, low, high, rows_y, own0))

    mirror_a = lax.ppermute(first[:PART], "gx", opposite)
    own0 = send(own0)
    rows_x = swap_y([low, high], g, 16)
    fixed_y = rows_y[:tile_x]
    moving_y = jnp.concatenate([rows_x[:1], rows_y[tile_x:], rows_x[1:]])
    column = columns(table, tab, low, moving, high, moving_y)
    shells = shell_rows(low, moving, high, moving_y, column, g)
    own1 = pack(table, tab, 1, False, [moving], shells)
    mirror_a, own0, own1, shells, rest = hold((mirror_a, own0, own1, shells, first[PART:]))

    mirror_b = lax.ppermute(rest, "gx", opposite)
    shells_far = lax.ppermute(shells, "gx", opposite)
    own1 = send(own1)
    mirror_b, shells_far, own1 = hold((mirror_b, shells_far, own1))

    far0 = send(pack(table, tab, 0, True, [mirror_a, mirror_b]))
    far1 = pack(table, tab, 1, True, [mirror_a, mirror_b], shells_far)
    _, far1 = hold((far0, far1))
    far1 = send(far1)

    warped = pick(table, tab, 0, own0, far0, fixed.shape)
    warped_y = swap_y([warped], g, 16)
    faces_x = shift_x([(warped, warped_y), (fixed, fixed_y)], 5)
    field = inner(table, tab, weights, warped, warped_y, fixed, fixed_y)
    field = rim(table, tab, weights, field, warped, warped_y, fixed, fixed_y, (*faces_x, *faces_x))
    field_y = swap_y([field], g, 8)
    field_x = shift_x([(field, field_y)], 4)

    mismatch = warp(table, tab, 1, own1, far1, fixed, field)
    mismatch_y = swap_y([mismatch], g, 8)
    mismatch_x = shift_x([(mismatch, mismatch_y)], 5)
    last = inner(table, tab, weights, mismatch, mismatch_y, fixed, fixed_y, field, field_y)
    last = rim(
        table, tab, weights, last, mismatch, mismatch_y, fixed, fixed_y, (*mismatch_x, *faces_x), field, field_y, field_x
    )
    return (last, mismatch)


def solution(mesh):
    return jax.shard_map(
        local,
        mesh=mesh,
        in_specs=(
            P(("groups", "gx"), "gy", None),
            P(("groups", "gx"), "gy", None),
            P("groups", None, None, None),
            P("groups", None, None, None),
        ),
        out_specs=(P(None, ("groups", "gx"), "gy", None), P(("groups", "gx"), "gy", None)),
        check_vma=False,
    )
```
